32 devices in a mesh: nodes: 8 (over z, y), feat: 4 (over x, core).
Axes of the slice: x: 2, y: 2, z: 4, core: 2. Of those that a mesh axis runs over, the one named last changes fastest.
Arguments:
- features: bfloat16 [32768, 1024], P('nodes', 'feat'), may hold values from -6 to 6
- pair_count: int32 [8, 8], P('nodes'), may hold values from 1 to 2, as said below
- send_blocks: int32 [8, 8, 2], P('nodes'), may hold values from 0 to 31
- tile_src: int32 [256, 4], P('nodes'), may hold values from 0 to 15, as said below
- tiles: bfloat16 [256, 4, 128, 128], P('nodes'), may hold values from -0.25 to 0.25
- labels: int32 [32768], P('nodes'), may hold values from 0 to 15
- w_first: bfloat16 [1024, 1024], P('feat'), may hold values from -0.1875 to 0.1875
- b_first: float32 [1024], P('feat'), may hold values from -3 to 3
- w_second: bfloat16 [1024, 16], P('feat'), may hold values from -0.1875 to 0.1875
Outputs:
- grad_first: float32 [1024, 1024], P('feat', 'nodes')
- grad_bias: float32 [1024], P('feat')
- grad_second: float32 [1024, 16], P('feat')
The draws below stay inside these ranges and needn't reach their ends.
Inputs may be any that keep to these rules, and one draw needn't show every extreme that they name: pair_count[p, p] is 2 for every p. `tile_src`: the 32 rows of one partition name every slot 0 to 15 at least once.
All inputs are finite; a program needn't handle non-finite values.
Results may differ from the reference program's by a relative error of at most 0.015.
The reference program's roundings to bfloat16 on the way count: a program that leaves them out, or rounds other values in their place, can miss the bound.
Values may be sent and summed in bfloat16 or wider, within the bound.
A program may use at most 128 MiB of HBM per device.

```python
import jax
import jax.numpy as jnp
from jax import lax

D = 1024
H = 1024
C = 16
BLK = 128
SLOTS = 2
PARTS_SIZE = 8
NB = 32
TPB = 4
NBLK = 256
NODES = 32768


def draw_pair_count(key, part):
    key = jax.random.fold_in(key, 11)
    counts = jax.random.randint(key, (PARTS_SIZE, PARTS_SIZE), 1, SLOTS + 1)
    diag = jnp.arange(PARTS_SIZE)[:, None] == jnp.arange(PARTS_SIZE)[None, :]
    return jnp.where(diag, SLOTS, counts).astype(jnp.int32)


def draw_tile_src(key, part):
    key = jax.random.fold_in(key, 23)
    keys = jax.random.split(key, PARTS_SIZE)

    def single(sub):
        order = jax.random.permutation(sub, NB * TPB)
        return (order % (PARTS_SIZE * SLOTS)).reshape(NB, TPB)
    return jax.vmap(single)(keys).reshape(NBLK, TPB).astype(jnp.int32)


def set_ends(result, rng, smallest, high):
    longest = result.shape.index(max(result.shape))
    spots = []
    for shift in (0, 1):
        where = [jax.random.randint(jax.random.fold_in(rng, axis), (), 0, length) for axis, length in enumerate(result.shape)]
        where[longest] = (where[longest] + shift) % result.shape[longest]
        spots.append(tuple(where))
    return result.at[spots[0]].set(smallest).at[spots[1]].set(high)


def block_scale(rng, extent, shards, low, top_value):
    def one(axis_at, parts):
        heights = jax.random.uniform(jax.random.fold_in(jax.random.fold_in(rng, 6), axis_at), (parts,), jnp.float32, low / len(shards), top_value / len(shards))
        return jnp.repeat(jnp.exp(heights), extent[axis_at] // parts).reshape((-1,) + (1,) * (len(extent) - axis_at - 1))

    loudness = one(*shards[0])
    for cut in shards[1:]:
        loudness = loudness * one(*cut)
    return loudness


def gaussian(key, extent, deviation, reach, pieces=(), kind=jnp.bfloat16):
    factor_of = block_scale(key, extent, pieces, -0.22, 0.18) if pieces else 1.0
    result = jax.random.normal(key, extent, jnp.float32) * deviation * factor_of
    return jnp.minimum(jnp.maximum(result, -reach), reach).astype(kind)


def setup_inputs(seed: int = 0) -> dict:
    streams_of = jax.random.split(jax.random.key(seed), 10)
    return {
        "features": gaussian(streams_of[0], (NODES, D), 1.0, 6.0, ((0, 8), (1, 4))),
        "pair_count": draw_pair_count(jax.random.fold_in(streams_of[9], 71), 0),
        "send_blocks": set_ends(jax.random.randint(streams_of[2], (PARTS_SIZE, PARTS_SIZE, SLOTS), 0, NB), jax.random.fold_in(streams_of[2], 1), 0, NB - 1).astype(jnp.int32),
        "tile_src": draw_tile_src(jax.random.fold_in(streams_of[9], 71), 0),
        "tiles": gaussian(streams_of[4], (NBLK, TPB, BLK, BLK), (TPB * BLK) ** -0.5, 0.25, ((0, 8),)),
        "labels": set_ends(jax.random.randint(streams_of[5], (NODES,), 0, C), jax.random.fold_in(streams_of[5], 1), 0, C - 1).astype(jnp.int32),
        "w_first": gaussian(streams_of[6], (D, H), D ** -0.5, 0.1875, ((0, 4),)),
        "b_first": gaussian(streams_of[7], (H,), 0.5, 3.0, ((0, 4),), jnp.float32),
        "w_second": gaussian(streams_of[8], (H, C), H ** -0.5, 0.1875, ((0, 4),)),
    }


def reference(features, pair_count, send_blocks, tile_src, tiles, labels, w_first, b_first, w_second):
    high = lax.Precision.HIGHEST
    part_ids = jnp.arange(PARTS_SIZE, dtype=jnp.int32)
    tiles_part = tiles.reshape(PARTS_SIZE, NB, TPB, BLK, BLK)
    source_part = tile_src.reshape(PARTS_SIZE, NB, TPB)

    def weights_of(p):
        slot = source_part[p] % SLOTS
        owner = source_part[p] // SLOTS
        live = (slot < pair_count[p][owner]).astype(jnp.float32)
        return tiles_part[p].astype(jnp.float32) * live[:, :, None, None]

    def incoming(field, p):
        blocks = send_blocks[:, p, :]
        received = field[part_ids[:, None], blocks]
        width = field.shape[-1]
        return received.reshape(PARTS_SIZE * SLOTS, BLK, width)[source_part[p]]
    field_one = features.reshape(PARTS_SIZE, NB, BLK, D)

    def first_agg(p):
        source = incoming(field_one, p).astype(jnp.float32)
        summed = jnp.einsum('btij,btjf->bif', weights_of(p), source, precision=high)
        return (field_one[p].astype(jnp.float32) + summed).astype(jnp.bfloat16)
    agg_first = lax.map(first_agg, part_ids).reshape(NODES, D)
    pre = jnp.dot(agg_first, w_first, preferred_element_type=jnp.float32) + b_first
    hidden = jnp.maximum(pre, 0.0).astype(jnp.bfloat16)
    proj = jnp.dot(hidden, w_second, preferred_element_type=jnp.float32)
    field_two = proj.reshape(PARTS_SIZE, NB, BLK, C)

    def second_agg(p):
        source = incoming(field_two, p)
        return field_two[p] + jnp.einsum('btij,btjf->bif', weights_of(p), source, precision=high)
    logits = lax.map(second_agg, part_ids).reshape(NODES, C)
    expo = jnp.exp(logits)
    probs = expo / lax.optimization_barrier(jnp.sum(expo, axis=1, keepdims=True))
    onehot = (labels[:, None] == jnp.arange(C, dtype=jnp.int32)[None, :]).astype(jnp.float32)
    dlog = (probs - onehot) / jnp.sqrt(jnp.float32(NODES))
    dlog_b = dlog.astype(jnp.bfloat16).reshape(PARTS_SIZE, NB, BLK, C)

    def back_step(total, p):
        contrib = jnp.einsum('btij,bif->btjf', weights_of(p), dlog_b[p].astype(jnp.float32), precision=high)
        slotsum = jnp.zeros((PARTS_SIZE * SLOTS, BLK, C), jnp.float32)
        slotsum = slotsum.at[source_part[p].reshape(-1)].add(contrib.reshape(NB * TPB, BLK, C))
        total = total.at[part_ids[:, None], send_blocks[:, p, :]].add(slotsum.reshape(PARTS_SIZE, SLOTS, BLK, C))
        return (total, 0)
    spread, unused = lax.scan(back_step, jnp.zeros((PARTS_SIZE, NB, BLK, C), jnp.float32), part_ids)
    dproj = dlog + spread.reshape(NODES, C)
    dproj_b = dproj.astype(jnp.bfloat16)
    grad_second = jnp.dot(hidden.T, dproj_b, preferred_element_type=jnp.float32)
    dhid = jnp.dot(dproj_b, w_second.T, preferred_element_type=jnp.float32)
    dpre = jnp.where(pre > 0, dhid, jnp.float32(0.0))
    grad_bias = lax.optimization_barrier(jnp.sum(dpre, axis=0))
    grad_first = jnp.dot(agg_first.T, dpre.astype(jnp.bfloat16), preferred_element_type=jnp.float32)
    return (grad_first, grad_bias, grad_second)
```

```python
import math

import jax
import jax.numpy as jnp
from jax import lax
from jax.sharding import PartitionSpec as P


def shards(features, pair_count, send_blocks, tile_src, tiles, labels, w_first, b_first, w_second):
    high = lax.Precision.HIGHEST
    rows, width = features.shape
    nblocks, per_block = tile_src.shape
    blk = tiles.shape[2]
    parts = lax.axis_size("nodes")
    fsize = lax.axis_size("feat")
    me = lax.axis_index("feat")
    slots = send_blocks.shape[2]
    grades = w_second.shape[1]
    mine = nblocks // fsize
    mrows = rows // fsize
    live = (tile_src % slots) < pair_count[0][tile_src // slots]
    weights = tiles * live[:, :, None, None].astype(jnp.bfloat16)
    table = send_blocks[0]

    w1 = lax.all_gather(w_first, "feat", axis=0, tiled=True)
    w2 = lax.all_gather(w_second, "feat", axis=0, tiled=True)
    b1 = lax.all_gather(b_first, "feat", axis=0, tiled=True)

    own_one = features.reshape(nblocks, blk, width)
    arrived = lax.all_to_all(own_one[table], "nodes", split_axis=0, concat_axis=0, tiled=True)
    sources = arrived.reshape(parts * slots, blk, width)[tile_src]
    summed = jnp.einsum("btij,btjf->bif", weights, sources, preferred_element_type=jnp.float32)
    agg = (summed + own_one).astype(jnp.bfloat16).reshape(rows, width)
    agg = lax.all_to_all(agg, "feat", split_axis=0, concat_axis=1, tiled=True)
    pre = jnp.dot(agg, w1, preferred_element_type=jnp.float32) + b1
    hidden = jnp.maximum(pre, 0.0).astype(jnp.bfloat16)
    proj = jnp.dot(hidden, w2, preferred_element_type=jnp.float32)

    proj_part = lax.all_gather(proj, "feat", axis=0, tiled=True).reshape(nblocks, blk, grades)
    arrived_two = lax.all_to_all(proj_part[table], "nodes", split_axis=0, concat_axis=0, tiled=True)
    my_src = lax.dynamic_slice_in_dim(tile_src, me * mine, mine, 0)
    my_w = lax.dynamic_slice_in_dim(weights, me * mine, mine, 0).astype(jnp.float32)
    my_labels = lax.dynamic_slice_in_dim(labels, me * mrows, mrows, 0)
    src_two = arrived_two.reshape(parts * slots, blk, grades)[my_src]
    logits = (jnp.einsum("btij,btjf->bif", my_w, src_two, precision=high)).reshape(mrows, grades) + proj
    expo = jnp.exp(logits)
    probs = expo / jnp.sum(expo, axis=1, keepdims=True)
    onehot = (my_labels[:, None] == jnp.arange(grades, dtype=jnp.int32)[None, :]).astype(jnp.float32)
    dlog = (probs - onehot) * (1.0 / math.sqrt(rows * parts))
    dlog_b = dlog.astype(jnp.bfloat16).reshape(mine, blk, grades)
    contrib = jnp.einsum(
        "btij,bif->btjf", my_w.astype(jnp.bfloat16), dlog_b, preferred_element_type=jnp.float32
    )
    slot_hit = (
        my_src.reshape(-1)[:, None] == jnp.arange(parts * slots, dtype=jnp.int32)[None, :]
    ).astype(jnp.float32)
    slotsum = lax.dot_general(
        slot_hit,
        contrib.reshape(mine * per_block, blk * grades),
        (((0,), (0,)), ((), ())),
        precision=high,
    )
    returned = lax.all_to_all(
        slotsum.reshape(parts, slots, blk, grades), "nodes", split_axis=0, concat_axis=0, tiled=True
    )
    placing = (table.reshape(-1)[None, :] == jnp.arange(nblocks, dtype=jnp.int32)[:, None]).astype(
        jnp.float32
    )
    spread = jnp.dot(placing, returned.reshape(parts * slots, blk * grades), precision=high)
    spread = lax.psum_scatter(spread, "feat", scatter_dimension=0, tiled=True)
    dproj_b = (dlog + spread.reshape(mrows, grades)).astype(jnp.bfloat16)
    grad_second = lax.dot_general(
        hidden, dproj_b, (((0,), (0,)), ((), ())), preferred_element_type=jnp.float32
    )
    dhid = lax.dot_general(dproj_b, w2, (((1,), (1,)), ((), ())), preferred_element_type=jnp.float32)
    dpre = jnp.where(pre > 0, dhid, 0.0)
    grad_bias = jnp.sum(dpre, axis=0)
    small = jnp.concatenate([grad_second, grad_bias[:, None]], axis=1)
    small = lax.psum(small, "nodes")
    small = lax.psum_scatter(small, "feat", scatter_dimension=0, tiled=True)
    grad_part = lax.dot_general(
        agg, dpre.astype(jnp.bfloat16), (((0,), (0,)), ((), ())), preferred_element_type=jnp.float32
    ).astype(jnp.bfloat16)
    grad_part = lax.psum_scatter(grad_part, "feat", scatter_dimension=0, tiled=True)
    grad_first = lax.psum_scatter(grad_part, "nodes", scatter_dimension=1, tiled=True)
    return (grad_first.astype(jnp.float32), small[:, grades], small[:, :grades])


def solution(mesh):
    placed = (
        P("nodes", "feat"),
        P("nodes", None),
        P("nodes", None, None),
        P("nodes", None),
        P("nodes", None, None, None),
        P("nodes"),
        P("feat", None),
        P("feat"),
        P("feat", None),
    )
    return jax.shard_map(
        shards,
        mesh=mesh,
        in_specs=placed,
        out_specs=(P("feat", "nodes"), P("feat"), P("feat", None)),
        check_vma=False,
    )
```

```python
import functools
import math

import jax
import jax.numpy as jnp
from jax import lax
from jax.experimental import pallas as pl
from jax.experimental.pallas import tpu as pltpu
from jax.sharding import PartitionSpec as P

MESH = pl.DeviceIdType.MESH
F32 = jnp.float32
BF16 = jnp.bfloat16


def flip(index, mask):
    bit = 1
    while bit <= mask:
        if mask & bit:
            index = index + bit - 2 * bit * ((index // bit) % 2)
        bit *= 2
    return index


def greet(parts, fsize, me_n, me_f):
    barrier = pltpu.get_barrier_semaphore()
    for d in range(1, fsize):
        pl.semaphore_signal(barrier, inc=1, device_id=(me_n, (me_f + d) % fsize), device_id_type=MESH)
    for d in range(1, parts):
        pl.semaphore_signal(barrier, inc=1, device_id=((me_n + d) % parts, me_f), device_id_type=MESH)
    pl.semaphore_wait(barrier, fsize + parts - 2)


def remote(src, dst, send, recv, device):
    return pltpu.make_async_remote_copy(
        src_ref=src, dst_ref=dst, send_sem=send, recv_sem=recv, device_id=device, device_id_type=MESH
    )


def stage_bits(parts, fsize):
    f_bits = [("f", 1 << i) for i in range(fsize.bit_length() - 1)]
    n_bits = [("n", 1 << i) for i in range(parts.bit_length() - 1)]
    first = f_bits + n_bits
    second = f_bits[:1] + n_bits[:1] + f_bits[1:] + n_bits[1:]
    return (first, second)


def kept(bits, done, fsize, parts):
    gone_f = sum(b for a, b in bits[:done] if a == "f")
    gone_n = sum(b for a, b in bits[:done] if a == "n")
    return [(f, n) for f in range(fsize) for n in range(parts) if not (f & gone_f) and not (n & gone_n)]


def later_kernel(
    dims, agg, w1, b1, w2, w2t, tiles, src, live, table, labels, grad_t, small_out,
    mask, mask_t, hidden, pall, sbuf, rbuf, r3, tl, dl, contrib, sback, rback, spread, rspread,
    dproj_t, dpre_t, acc, gout, gin, sm, smin, tile_sem,
    ag_s, ag_r, ex_s, ex_r, bk_s, bk_r, sp_s, sp_r, rs_s, rs_r, sm_s, sm_r,
):
    parts, fsize, slots, nblocks, per_block, blk, grades, scale = dims
    me_n, me_f = lax.axis_index("nodes"), lax.axis_index("feat")
    mine = nblocks // fsize
    rows, hid = hidden.shape
    width = rows // 4
    fw = agg.shape[1] // fsize
    hb = hid // parts
    half = fw // 2
    base = me_f * mine

    fetch = pltpu.make_async_copy(tiles.at[pl.ds(base, mine)], tl, tile_sem)
    fetch.start()
    greet(parts, fsize, me_n, me_f)

    @pl.loop(0, 4)
    def _(r):
        at = pl.ds(pl.multiple_of(r * width, width), width)
        pre = jnp.dot(agg[at, :], w1[...], preferred_element_type=F32) + b1[...]
        hb16 = jnp.maximum(pre, 0.0).astype(BF16)
        hidden[at, :] = hb16
        mask[at, :] = jnp.where(pre > 0, 1.0, 0.0).astype(BF16)
        pt = lax.dot_general(w2t[...], hb16, (((1,), (1,)), ((), ())), preferred_element_type=F32)
        for i in range(width // blk):
            pall[base + r * (width // blk) + i] = pt[:, i * blk : (i + 1) * blk]

    copies = []
    for d in range(1, fsize):
        own = pall.at[pl.ds(base, mine)]
        c = remote(own, own, ag_s.at[d], ag_r.at[d], (me_n, (me_f + d) % fsize))
        c.start()
        copies.append(c)
    fetch.wait()

    @pl.loop(0, 4)
    def _(r):
        at = pl.ds(pl.multiple_of(r * width, width), width)
        mask_t[:, at] = mask[at, :].T

    for c in copies:
        c.wait()
    for p in range(parts):
        for s in range(slots):
            sbuf[p, s] = pall[table[p, s]]
    rbuf[me_n] = sbuf[me_n]
    copies = []
    for d in range(1, parts):
        p = (me_n + d) % parts
        c = remote(sbuf.at[p], rbuf.at[me_n], ex_s.at[d], ex_r.at[d], (p, me_f))
        c.start()
        copies.append(c)
    for c in copies:
        c.wait()
    for p in range(parts):
        for s in range(slots):
            x = rbuf[p, s]
            hi = x.astype(BF16)
            rest = x - hi.astype(F32)
            mid = rest.astype(BF16)
            low = (rest - mid.astype(F32)).astype(BF16)
            r3[p * slots + s] = jnp.concatenate([hi, mid, low], axis=0)

    grade_id = lax.broadcasted_iota(jnp.int32, (grades, blk), 0)

    @pl.loop(0, mine)
    def _(b):
        pieces = [r3[src[base + b, k]] * live[base + b, k].astype(BF16) for k in range(per_block)]
        lhs = jnp.concatenate(pieces, axis=1)
        wcat = jnp.concatenate([tl[b, k] for k in range(per_block)], axis=1)
        out = lax.dot_general(lhs, wcat, (((1,), (1,)), ((), ())), preferred_element_type=F32)
        logits = pall[base + b] + (
            out[:grades] + (out[grades : 2 * grades] + out[2 * grades : 3 * grades])
        )
        expo = jnp.exp(logits)
        probs = expo / jnp.sum(expo, axis=0, keepdims=True)
        onehot = jnp.where(labels[pl.ds(base + b, 1), :] == grade_id, 1.0, 0.0)
        dlog = (probs - onehot) * scale
        dl[b] = dlog
        back = jnp.dot(dlog.astype(BF16), wcat, preferred_element_type=F32)
        for k in range(per_block):
            contrib[b * per_block + k] = back[:, k * blk : (k + 1) * blk] * live[base + b, k]

    @pl.loop(0, parts)
    def _(p):
        for s in range(slots):
            slot = p * slots + s
            total = jnp.zeros((grades, blk), F32)
            for b in range(mine):
                for k in range(per_block):
                    hit = jnp.where(src[base + b, k] == slot, 1.0, 0.0)
                    total = total + contrib[b * per_block + k] * hit
            sback[p, s] = total

    rback[me_n] = sback[me_n]
    copies = []
    for d in range(1, parts):
        p = (me_n + d) % parts
        c = remote(sback.at[p], rback.at[me_n], bk_s.at[d], bk_r.at[d], (p, me_f))
        c.start()
        copies.append(c)
    for c in copies:
        c.wait()

    @pl.loop(0, nblocks)
    def _(b):
        total = jnp.zeros((grades, blk), F32)
        for p in range(parts):
            for s in range(slots):
                hit = jnp.where(table[p, s] == b, 1.0, 0.0)
                total = total + rback[p, s] * hit
        spread[b] = total

    copies = []
    for d in range(1, fsize):
        to = (me_f + d) % fsize
        c = remote(
            spread.at[pl.ds(to * mine, mine)], rspread.at[d - 1], sp_s.at[d], sp_r.at[d], (me_n, to)
        )
        c.start()
        copies.append(c)
    for c in copies:
        c.wait()
    for b in range(mine):
        total = spread[base + b]
        for d in range(fsize - 1):
            total = total + rspread[d, b]
        dproj_t[:, b * blk : (b + 1) * blk] = (dl[b] + total).astype(BF16)

    for n in range(parts):
        at = pl.ds(pl.multiple_of(flip(me_n, n) * hb, hb), hb)
        d = jnp.dot(w2[at, :], dproj_t[...], preferred_element_type=F32)
        dpre_t[n * hb : (n + 1) * hb, :] = jnp.where(mask_t[at, :] > 0, d, 0.0).astype(BF16)

    orders = stage_bits(parts, fsize)
    stages = len(orders[0])
    sizes = [(fsize * parts) >> (t + 1) for t in range(stages)]
    starts = [sum(sizes[:t]) for t in range(stages)]

    def product(f):
        at = pl.ds(pl.multiple_of(flip(me_f, f) * fw, fw), fw)
        return jnp.dot(dpre_t[...], agg[:, at], preferred_element_type=F32)

    def partner(axis, bit):
        return (flip(me_n, bit), me_f) if axis == "n" else (me_n, flip(me_f, bit))

    def launch(c, t):
        at = pl.ds(starts[t], sizes[t])
        r = remote(gout.at[c, at], gin.at[c, at], rs_s.at[c, t], rs_r.at[c, t], partner(*orders[c][t]))
        r.start()
        return r

    def going(c, t):
        axis, bit = orders[c][t]
        return [j for j in kept(orders[c], t, fsize, parts) if (j[0] if axis == "f" else j[1]) & bit]

    flying = [None, None]
    for f in range(fsize):
        if f & 1:
            g = product(f).astype(BF16)
            for c in range(2):
                for i, j in enumerate(going(c, 0)):
                    if j[0] == f:
                        gout[c, i] = g[j[1] * hb : (j[1] + 1) * hb, c * half : (c + 1) * half]
    for c in range(2):
        flying[c] = launch(c, 0)
    for f in range(fsize):
        if not f & 1:
            g = product(f)
            for c in range(2):
                for n in range(parts):
                    acc[c, f, n] = g[n * hb : (n + 1) * hb, c * half : (c + 1) * half]

    both = jnp.dot(dproj_t[...], hidden[...], preferred_element_type=F32)
    bias = jnp.sum(
        w2t[...].astype(F32) * jnp.dot(dproj_t[...], mask[...], preferred_element_type=F32),
        axis=0,
        keepdims=True,
    )
    small_full = jnp.concatenate([both, jnp.broadcast_to(bias, (8, hid))], axis=0)
    rel = [small_full[:, g * fw : (g + 1) * fw] for g in range(fsize)]
    for f in range(fsize):
        pick = flip(me_f, f)
        total = rel[0]
        for g in range(1, fsize):
            total = jnp.where(pick == g, rel[g], total)
        sm[f] = total

    small_bits = orders[0]
    at_small = 0
    for t in range(stages):
        axis, bit = small_bits[t]
        if axis == "f":
            idx = [f for f in range(fsize) if not f & (bit - 1) and f & bit]
        else:
            idx = [0]
        smalls = []
        for f in idx:
            r = remote(sm.at[f], smin.at[at_small], sm_s.at[at_small], sm_r.at[at_small], partner(axis, bit))
            r.start()
            smalls.append((f - bit if axis == "f" else 0, at_small, r))
            at_small += 1
        for c in range(2):
            flying[c].wait()
            sent = going(c, t)
            axis_c, bit_c = orders[c][t]
            for i, j in enumerate(sent):
                k = (j[0] - bit_c, j[1]) if axis_c == "f" else (j[0], j[1] - bit_c)
                new = acc[c, k[0], k[1]] + gin[c, starts[t] + i].astype(F32)
                nxt = going(c, t + 1) if t + 1 < stages else []
                if k in nxt:
                    gout[c, starts[t + 1] + nxt.index(k)] = new.astype(BF16)
                elif t + 1 < stages:
                    acc[c, k[0], k[1]] = new
                else:
                    grad_t[:, c * half : (c + 1) * half] = new
            if t + 1 < stages:
                flying[c] = launch(c, t + 1)
        for _, _, r in smalls:
            r.wait()
        for f, slot, _ in smalls:
            sm[f] = sm[f] + smin[slot]
    small_out[...] = sm[0]


def later(dims, agg, w1, b1, w2, tiles, src, live, table, labels):
    parts, fsize, slots, nblocks, per_block, blk, grades, scale = dims
    mine = nblocks // fsize
    rows, feats = agg.shape
    hid = w1.shape[1]
    fw, hb = feats // fsize, hid // parts
    stages = len(stage_bits(parts, fsize)[0])
    tiles_sent = fsize * parts - 1
    n_small = (fsize - 1) + (parts.bit_length() - 1)
    vm = pl.BlockSpec(memory_space=pltpu.VMEM)
    sc = pl.BlockSpec(memory_space=pltpu.SMEM)
    dma = pltpu.SemaphoreType.DMA
    field = (grades, blk)
    return pl.pallas_call(
        functools.partial(later_kernel, dims),
        out_shape=(
            jax.ShapeDtypeStruct((hb, fw), F32),
            jax.ShapeDtypeStruct((grades + 8, fw), F32),
        ),
        in_specs=[vm, vm, vm, vm, vm, pl.BlockSpec(memory_space=pl.ANY), sc, sc, sc, vm],
        out_specs=(vm, vm),
        scratch_shapes=[
            pltpu.VMEM((rows, hid), BF16),
            pltpu.VMEM((hid, rows), BF16),
            pltpu.VMEM((rows, hid), BF16),
            pltpu.VMEM((nblocks,) + field, F32),
            pltpu.VMEM((parts, slots) + field, F32),
            pltpu.VMEM((parts, slots) + field, F32),
            pltpu.VMEM((parts * slots, 3 * grades, blk), BF16),
            pltpu.VMEM((mine, per_block, blk, blk), BF16),
            pltpu.VMEM((mine,) + field, F32),
            pltpu.VMEM((mine * per_block,) + field, F32),
            pltpu.VMEM((parts, slots) + field, F32),
            pltpu.VMEM((parts, slots) + field, F32),
            pltpu.VMEM((nblocks,) + field, F32),
            pltpu.VMEM((fsize - 1, mine) + field, F32),
            pltpu.VMEM((grades, rows), BF16),
            pltpu.VMEM((hid, rows), BF16),
            pltpu.VMEM((2, fsize, parts, hb, fw // 2), F32),
            pltpu.VMEM((2, tiles_sent, hb, fw // 2), BF16),
            pltpu.VMEM((2, tiles_sent, hb, fw // 2), BF16),
            pltpu.VMEM((fsize, grades + 8, fw), F32),
            pltpu.VMEM((n_small, grades + 8, fw), F32),
            dma,
            dma((fsize,)), dma((fsize,)),
            dma((parts,)), dma((parts,)),
            dma((parts,)), dma((parts,)),
            dma((fsize,)), dma((fsize,)),
            dma((2, stages)), dma((2, stages)),
            dma((n_small,)), dma((n_small,)),
        ],
        compiler_params=pltpu.CompilerParams(
            collective_id=1, has_side_effects=True, vmem_limit_bytes=56 * 1024 * 1024
        ),
        cost_estimate=pl.CostEstimate(
            flops=4 * rows * hid * feats, bytes_accessed=6 * rows * hid, transcendentals=rows * grades
        ),
    )(agg, w1, b1, w2, w2.T, tiles, src, live, table, labels)


def shards(features, pair_count, send_blocks, tile_src, tiles, labels, w_first, b_first, w_second):
    rows, width = features.shape
    nblocks, per_block = tile_src.shape
    blk = tiles.shape[2]
    parts = lax.axis_size("nodes")
    fsize = lax.axis_size("feat")
    slots = send_blocks.shape[2]
    grades = w_second.shape[1]
    live = (tile_src % slots) < pair_count[0][tile_src // slots]
    weights = tiles * live[:, :, None, None].astype(BF16)
    table = send_blocks[0]

    w1 = lax.all_gather(w_first, "feat", axis=0, tiled=True)
    w2 = lax.all_gather(w_second, "feat", axis=0, tiled=True)
    b1 = lax.all_gather(b_first, "feat", axis=0, tiled=True)

    own_one = features.reshape(nblocks, blk, width)
    arrived = lax.all_to_all(own_one[table], "nodes", split_axis=0, concat_axis=0, tiled=True)
    sources = arrived.reshape(parts * slots, blk, width)[tile_src]
    summed = jnp.einsum("btij,btjf->bif", weights, sources, preferred_element_type=F32)
    agg = (summed + own_one).astype(BF16).reshape(rows, width)
    agg = lax.all_to_all(agg, "feat", split_axis=0, concat_axis=1, tiled=True)

    dims = (parts, fsize, slots, nblocks, per_block, blk, grades, 1.0 / math.sqrt(rows * parts))
    grad_t, small = later(
        dims, agg, w1, b1[None, :], w2, tiles, tile_src, live.astype(F32), table,
        labels.reshape(nblocks, blk),
    )
    return (grad_t.T, small[grades], small[:grades].T)


def solution(mesh):
    placed = (
        P("nodes", "feat"),
        P("nodes", None),
        P("nodes", None, None),
        P("nodes", None),
        P("nodes", None, None, None),
        P("nodes"),
        P("feat", None),
        P("feat"),
        P("feat", None),
    )
    return jax.shard_map(
        shards,
        mesh=mesh,
        in_specs=placed,
        out_specs=(P("feat", "nodes"), P("feat"), P("feat", None)),
        check_vma=False,
    )
```

```python
import functools
import math

import jax
import jax.numpy as jnp
from jax import lax
from jax.experimental import pallas as pl
from jax.experimental.pallas import tpu as pltpu
from jax.sharding import PartitionSpec as P

MESH = pl.DeviceIdType.MESH
F32 = jnp.float32
BF16 = jnp.bfloat16


def flip(index, mask):
    bit = 1
    while bit <= mask:
        if mask & bit:
            index = index + bit - 2 * bit * ((index // bit) % 2)
        bit *= 2
    return index


def greet(parts, fsize, me_n, me_f):
    barrier = pltpu.get_barrier_semaphore()
    for d in range(1, fsize):
        pl.semaphore_signal(barrier, inc=1, device_id=(me_n, (me_f + d) % fsize), device_id_type=MESH)
    for d in range(1, parts):
        pl.semaphore_signal(barrier, inc=1, device_id=((me_n + d) % parts, me_f), device_id_type=MESH)
    pl.semaphore_wait(barrier, fsize + parts - 2)


def remote(src, dst, send, recv, device):
    return pltpu.make_async_remote_copy(
        src_ref=src, dst_ref=dst, send_sem=send, recv_sem=recv, device_id=device, device_id_type=MESH
    )


def stage_bits(parts, fsize):
    f_bits = [("f", 1 << i) for i in range(fsize.bit_length() - 1)]
    n_bits = [("n", 1 << i) for i in range(parts.bit_length() - 1)]
    first = f_bits + n_bits
    second = f_bits[:1] + n_bits[:1] + f_bits[1:] + n_bits[1:]
    return (first, second)


def kept(bits, done, fsize, parts):
    gone_f = sum(b for a, b in bits[:done] if a == "f")
    gone_n = sum(b for a, b in bits[:done] if a == "n")
    return [(f, n) for f in range(fsize) for n in range(parts) if not (f & gone_f) and not (n & gone_n)]


def whole_kernel(
    dims, feats_in, w_in, b_in, w2_in, tiles, src, count, table, labels, grad_out, bias_out, second_out,
    agg, w1, w2, b_all, w2t, b1, fsend, frecv_a, frecv_b, abuf,
    mask, mask_t, hidden, pall, sbuf, rbuf, r3, tl, dl, contrib, sback, rback, spread, rspread,
    dproj_t, dpre_t, acc, gout, gin, sm, smin, tile_sem,
    w_s, w_r, w2_s, w2_r, b_s, b_r, fx_s, fx_r, tr_s, tr_r,
    ag_s, ag_r, ex_s, ex_r, bk_s, bk_r, sp_s, sp_r, rs_s, rs_r, sm_s, sm_r,
):
    parts, fsize, slots, nblocks, per_block, blk, grades, scale = dims
    me_n, me_f = lax.axis_index("nodes"), lax.axis_index("feat")
    mine = nblocks // fsize
    rows, hid = hidden.shape
    width = rows // 4
    fw = agg.shape[1] // fsize
    hb = hid // parts
    half = fw // 2
    base = me_f * mine

    def live(b, k):
        slot = src[b, k]
        return jnp.where(slot % slots < count[0, slot // slots], 1.0, 0.0)

    fetch = pltpu.make_async_copy(tiles, tl, tile_sem)
    fetch.start()
    frecv = (frecv_a, frecv_b)
    own_w = pl.ds(pl.multiple_of(me_f * fw, fw), fw)
    w1[own_w, :] = w_in[...]
    w2[own_w, :] = jnp.zeros((fw, blk), BF16)
    w2[own_w, :grades] = w2_in[...]
    b_all[me_f] = jnp.broadcast_to(b_in[...], (8, fw))
    greet(parts, fsize, me_n, me_f)

    def column(c):
        return slice(c * half, (c + 1) * half)

    def exchange(c, d):
        p = (me_n + d) % parts
        return remote(fsend.at[c, p], frecv[c].at[me_n], fx_s.at[c, d], fx_r.at[c, d], (p, me_f))

    def stage_block(c, p, s):
        fsend[c, p, s] = feats_in[table[0, p, s], :, column(c)]

    for p in range(parts):
        for s in range(slots):
            stage_block(0, p, s)
    first = []
    for d in range(1, parts):
        x = exchange(0, d)
        x.start()
        first.append(x)

    def pass_on(j, bit, slot):
        at = pl.ds(pl.multiple_of(flip(me_f, j) * fw, fw), fw)
        return remote(w1.at[at, :], w1.at[at, :], w_s.at[slot], w_r.at[slot], (me_n, flip(me_f, bit)))

    weights_flying = []
    far = []
    for j in range(1, fsize):
        if j & (j - 1) == 0:
            x = pass_on(0, j, j)
            x.start()
            (far if j > 1 else weights_flying).append(x)
    for d in range(1, fsize):
        to = (me_n, (me_f + d) % fsize)
        x = remote(w2.at[own_w, :], w2.at[own_w, :], w2_s.at[d], w2_r.at[d], to)
        x.start()
        y = remote(b_all.at[me_f], b_all.at[me_f], b_s.at[d], b_r.at[d], to)
        y.start()
        weights_flying += [x, y]

    for p in range(parts):
        for s in range(slots):
            stage_block(1, p, s)
    frecv_a[me_n] = fsend[0, me_n]
    frecv_b[me_n] = fsend[1, me_n]
    second = []
    for d in range(1, parts):
        first[d - 1].wait_send()
        x = exchange(1, d)
        x.start()
        second.append(x)
    fetch.wait()
    for x in first:
        x.wait_recv()

    order = list(range(fsize - 1, -1, -1))

    def aggregate(c):
        def block(b):
            wcat = jnp.concatenate([tl[b, k] * live(b, k).astype(BF16) for k in range(per_block)], axis=1)
            got = jnp.concatenate(
                [frecv[c][src[b, k] // slots, src[b, k] % slots] for k in range(per_block)], axis=0
            )
            total = jnp.dot(wcat, got, preferred_element_type=F32)
            return (total + feats_in[b, :, column(c)].astype(F32)).astype(BF16)

        lanes = pl.ds(pl.multiple_of(me_f * fw + c * half, half), half)
        sent = []
        for j in order:
            group = flip(me_f, j)

            @pl.loop(0, mine)
            def _(i):
                got = block(group * mine + i)
                if j:
                    abuf[c, pl.ds(pl.multiple_of((group * mine + i) * blk, blk), blk), :] = got
                else:
                    agg[pl.ds(pl.multiple_of(i * blk, blk), blk), lanes] = got

            if j:
                at = pl.ds(pl.multiple_of(group * rows, rows), rows)
                x = remote(abuf.at[c, at, :], agg.at[:, lanes], tr_s.at[c, j], tr_r.at[c, j], (me_n, group))
                x.start()
                sent.append(x)
        return sent

    turned = aggregate(0)
    for x in far:
        x.wait()
    for j in range(3, fsize):
        low = j & -j
        if j != low:
            x = pass_on(j - low, low, j)
            x.start()
            weights_flying.append(x)
    for x in second:
        x.wait()
    turned += aggregate(1)
    for x in weights_flying:
        x.wait()
    for f in range(fsize):
        b1[:, f * fw : (f + 1) * fw] = b_all[f, :1, :]
    w2t[...] = w2[...].T[:grades]
    for x in turned:
        x.wait()

    @pl.loop(0, 4)
    def _(r):
        at = pl.ds(pl.multiple_of(r * width, width), width)
        pre = jnp.dot(agg[at, :], w1[...], preferred_element_type=F32) + b1[...]
        hb16 = jnp.maximum(pre, 0.0).astype(BF16)
        hidden[at, :] = hb16
        mask[at, :] = jnp.where(pre > 0, 1.0, 0.0).astype(BF16)
        pt = lax.dot_general(w2t[...], hb16, (((1,), (1,)), ((), ())), preferred_element_type=F32)
        for i in range(width // blk):
            pall[base + r * (width // blk) + i] = pt[:, i * blk : (i + 1) * blk]

    copies = []
    for d in range(1, fsize):
        own = pall.at[pl.ds(base, mine)]
        c = remote(own, own, ag_s.at[d], ag_r.at[d], (me_n, (me_f + d) % fsize))
        c.start()
        copies.append(c)

    @pl.loop(0, 4)
    def _(r):
        at = pl.ds(pl.multiple_of(r * width, width), width)
        mask_t[:, at] = mask[at, :].T

    for c in copies:
        c.wait()
    for p in range(parts):
        for s in range(slots):
            sbuf[p, s] = pall[table[0, p, s]]
    rbuf[me_n] = sbuf[me_n]
    copies = []
    for d in range(1, parts):
        p = (me_n + d) % parts
        c = remote(sbuf.at[p], rbuf.at[me_n], ex_s.at[d], ex_r.at[d], (p, me_f))
        c.start()
        copies.append(c)
    for c in copies:
        c.wait()
    for p in range(parts):
        for s in range(slots):
            x = rbuf[p, s]
            hi = x.astype(BF16)
            rest = x - hi.astype(F32)
            mid = rest.astype(BF16)
            low = (rest - mid.astype(F32)).astype(BF16)
            r3[p * slots + s] = jnp.concatenate([hi, mid, low], axis=0)

    grade_id = lax.broadcasted_iota(jnp.int32, (grades, blk), 0)

    @pl.loop(0, mine)
    def _(b):
        pieces = [r3[src[base + b, k]] * live(base + b, k).astype(BF16) for k in range(per_block)]
        lhs = jnp.concatenate(pieces, axis=1)
        wcat = jnp.concatenate([tl[base + b, k] for k in range(per_block)], axis=1)
        out = lax.dot_general(lhs, wcat, (((1,), (1,)), ((), ())), preferred_element_type=F32)
        logits = pall[base + b] + (
            out[:grades] + (out[grades : 2 * grades] + out[2 * grades : 3 * grades])
        )
        expo = jnp.exp(logits)
        probs = expo / jnp.sum(expo, axis=0, keepdims=True)
        onehot = jnp.where(labels[pl.ds(base + b, 1), :] == grade_id, 1.0, 0.0)
        dlog = (probs - onehot) * scale
        dl[b] = dlog
        back = jnp.dot(dlog.astype(BF16), wcat, preferred_element_type=F32)
        for k in range(per_block):
            contrib[b * per_block + k] = back[:, k * blk : (k + 1) * blk] * live(base + b, k)

    @pl.loop(0, parts)
    def _(p):
        for s in range(slots):
            slot = p * slots + s
            total = jnp.zeros((grades, blk), F32)
            for b in range(mine):
                for k in range(per_block):
                    hit = jnp.where(src[base + b, k] == slot, 1.0, 0.0)
                    total = total + contrib[b * per_block + k] * hit
            sback[p, s] = total

    rback[me_n] = sback[me_n]
    copies = []
    for d in range(1, parts):
        p = (me_n + d) % parts
        c = remote(sback.at[p], rback.at[me_n], bk_s.at[d], bk_r.at[d], (p, me_f))
        c.start()
        copies.append(c)
    for c in copies:
        c.wait()

    @pl.loop(0, nblocks)
    def _(b):
        total = jnp.zeros((grades, blk), F32)
        for p in range(parts):
            for s in range(slots):
                hit = jnp.where(table[0, p, s] == b, 1.0, 0.0)
                total = total + rback[p, s] * hit
        spread[b] = total

    copies = []
    for d in range(1, fsize):
        to = (me_f + d) % fsize
        c = remote(
            spread.at[pl.ds(to * mine, mine)], rspread.at[d - 1], sp_s.at[d], sp_r.at[d], (me_n, to)
        )
        c.start()
        copies.append(c)
    for c in copies:
        c.wait()
    for b in range(mine):
        total = spread[base + b]
        for d in range(fsize - 1):
            total = total + rspread[d, b]
        dproj_t[:, b * blk : (b + 1) * blk] = (dl[b] + total).astype(BF16)

    for n in range(parts):
        at = pl.ds(pl.multiple_of(flip(me_n, n) * hb, hb), hb)
        d = jnp.dot(w2[at, :grades], dproj_t[...], preferred_element_type=F32)
        dpre_t[n * hb : (n + 1) * hb, :] = jnp.where(mask_t[at, :] > 0, d, 0.0).astype(BF16)

    orders = stage_bits(parts, fsize)
    stages = len(orders[0])
    sizes = [(fsize * parts) >> (t + 1) for t in range(stages)]
    starts = [sum(sizes[:t]) for t in range(stages)]

    def product(f):
        at = pl.ds(pl.multiple_of(flip(me_f, f) * fw, fw), fw)
        return jnp.dot(dpre_t[...], agg[:, at], preferred_element_type=F32)

    def partner(axis, bit):
        return (flip(me_n, bit), me_f) if axis == "n" else (me_n, flip(me_f, bit))

    def launch(c, t):
        at = pl.ds(starts[t], sizes[t])
        r = remote(gout.at[c, at], gin.at[c, at], rs_s.at[c, t], rs_r.at[c, t], partner(*orders[c][t]))
        r.start()
        return r

    def going(c, t):
        axis, bit = orders[c][t]
        return [j for j in kept(orders[c], t, fsize, parts) if (j[0] if axis == "f" else j[1]) & bit]

    flying = [None, None]
    for f in range(fsize):
        if f & 1:
            g = product(f).astype(BF16)
            for c in range(2):
                for i, j in enumerate(going(c, 0)):
                    if j[0] == f:
                        gout[c, i] = g[j[1] * hb : (j[1] + 1) * hb, c * half : (c + 1) * half]
    for c in range(2):
        flying[c] = launch(c, 0)
    for f in range(fsize):
        if not f & 1:
            g = product(f)
            for c in range(2):
                for n in range(parts):
                    acc[c, f, n] = g[n * hb : (n + 1) * hb, c * half : (c + 1) * half]

    both = jnp.dot(dproj_t[...], hidden[...], preferred_element_type=F32)
    bias = jnp.sum(
        w2t[...].astype(F32) * jnp.dot(dproj_t[...], mask[...], preferred_element_type=F32),
        axis=0,
        keepdims=True,
    )
    small_full = jnp.concatenate([both, jnp.broadcast_to(bias, (8, hid))], axis=0)
    rel = [small_full[:, g * fw : (g + 1) * fw] for g in range(fsize)]
    for f in range(fsize):
        pick = flip(me_f, f)
        total = rel[0]
        for g in range(1, fsize):
            total = jnp.where(pick == g, rel[g], total)
        sm[f] = total

    small_bits = orders[0]
    at_small = 0
    for t in range(stages):
        axis, bit = small_bits[t]
        if axis == "f":
            idx = [f for f in range(fsize) if not f & (bit - 1) and f & bit]
        else:
            idx = [0]
        smalls = []
        for f in idx:
            r = remote(sm.at[f], smin.at[at_small], sm_s.at[at_small], sm_r.at[at_small], partner(axis, bit))
            r.start()
            smalls.append((f - bit if axis == "f" else 0, at_small, r))
            at_small += 1
        for c in range(2):
            flying[c].wait()
            sent = going(c, t)
            axis_c, bit_c = orders[c][t]
            for i, j in enumerate(sent):
                k = (j[0] - bit_c, j[1]) if axis_c == "f" else (j[0], j[1] - bit_c)
                new = acc[c, k[0], k[1]] + gin[c, starts[t] + i].astype(F32)
                nxt = going(c, t + 1) if t + 1 < stages else []
                if k in nxt:
                    gout[c, starts[t + 1] + nxt.index(k)] = new.astype(BF16)
                elif t + 1 < stages:
                    acc[c, k[0], k[1]] = new
                else:
                    grad_out[c * half : (c + 1) * half, :] = new.T
            if t + 1 < stages:
                flying[c] = launch(c, t + 1)
        for _, _, r in smalls:
            r.wait()
        for f, slot, _ in smalls:
            sm[f] = sm[f] + smin[slot]
    bias_out[...] = sm[0, grades : grades + 1, :]
    second_out[...] = sm[0, :grades, :].T


def shards(features, pair_count, send_blocks, tile_src, tiles, labels, w_first, b_first, w_second):
    nodes, fw = features.shape
    nblocks, per_block = tile_src.shape
    blk = tiles.shape[2]
    parts = lax.axis_size("nodes")
    fsize = lax.axis_size("feat")
    slots = send_blocks.shape[2]
    grades = w_second.shape[1]
    mine = nblocks // fsize
    rows, feats, hid = nodes // fsize, fw * fsize, w_first.shape[1]
    hb = hid // parts
    half = fw // 2
    dims = (parts, fsize, slots, nblocks, per_block, blk, grades, 1.0 / math.sqrt(nodes * parts))
    stages = len(stage_bits(parts, fsize)[0])
    tiles_sent = fsize * parts - 1
    n_small = (fsize - 1) + (parts.bit_length() - 1)
    vm = pl.BlockSpec(memory_space=pltpu.VMEM)
    sc = pl.BlockSpec(memory_space=pltpu.SMEM)
    dma = pltpu.SemaphoreType.DMA
    field = (grades, blk)
    grad_first, grad_bias, grad_second = pl.pallas_call(
        functools.partial(whole_kernel, dims),
        out_shape=(
            jax.ShapeDtypeStruct((fw, hb), F32),
            jax.ShapeDtypeStruct((1, fw), F32),
            jax.ShapeDtypeStruct((fw, grades), F32),
        ),
        in_specs=[vm, vm, vm, vm, pl.BlockSpec(memory_space=pl.ANY), sc, sc, sc, vm],
        out_specs=(vm, vm, vm),
        scratch_shapes=[
            pltpu.VMEM((rows, feats), BF16),
            pltpu.VMEM((feats, hid), BF16),
            pltpu.VMEM((hid, blk), BF16),
            pltpu.VMEM((fsize, 8, fw), F32),
            pltpu.VMEM((grades, hid), BF16),
            pltpu.VMEM((1, hid), F32),
            pltpu.VMEM((2, parts, slots, blk, half), BF16),
            pltpu.VMEM((parts, slots, blk, half), BF16),
            pltpu.VMEM((parts, slots, blk, half), BF16),
            pltpu.VMEM((2, nodes, half), BF16),
            pltpu.VMEM((rows, hid), BF16),
            pltpu.VMEM((hid, rows), BF16),
            pltpu.VMEM((rows, hid), BF16),
            pltpu.VMEM((nblocks,) + field, F32),
            pltpu.VMEM((parts, slots) + field, F32),
            pltpu.VMEM((parts, slots) + field, F32),
            pltpu.VMEM((parts * slots, 3 * grades, blk), BF16),
            pltpu.VMEM((nblocks, per_block, blk, blk), BF16),
            pltpu.VMEM((mine,) + field, F32),
            pltpu.VMEM((mine * per_block,) + field, F32),
            pltpu.VMEM((parts, slots) + field, F32),
            pltpu.VMEM((parts, slots) + field, F32),
            pltpu.VMEM((nblocks,) + field, F32),
            pltpu.VMEM((fsize - 1, mine) + field, F32),
            pltpu.VMEM((grades, rows), BF16),
            pltpu.VMEM((hid, rows), BF16),
            pltpu.VMEM((2, fsize, parts, hb, half), F32),
            pltpu.VMEM((2, tiles_sent, hb, half), BF16),
            pltpu.VMEM((2, tiles_sent, hb, half), BF16),
            pltpu.VMEM((fsize, grades + 8, fw), F32),
            pltpu.VMEM((n_small, grades + 8, fw), F32),
            dma,
            dma((fsize,)), dma((fsize,)),
            dma((fsize,)), dma((fsize,)),
            dma((fsize,)), dma((fsize,)),
            dma((2, parts)), dma((2, parts)),
            dma((2, fsize)), dma((2, fsize)),
            dma((fsize,)), dma((fsize,)),
            dma((parts,)), dma((parts,)),
            dma((parts,)), dma((parts,)),
            dma((fsize,)), dma((fsize,)),
            dma((2, stages)), dma((2, stages)),
            dma((n_small,)), dma((n_small,)),
        ],
        compiler_params=pltpu.CompilerParams(
            collective_id=1, has_side_effects=True, vmem_limit_bytes=60 * 1024 * 1024
        ),
        cost_estimate=pl.CostEstimate(
            flops=4 * rows * hid * feats, bytes_accessed=6 * rows * hid, transcendentals=rows * grades
        ),
    )(
        features.reshape(nblocks, blk, fw), w_first, b_first[None, :], w_second, tiles, tile_src,
        pair_count, send_blocks, labels.reshape(nblocks, blk),
    )
    return (grad_first, grad_bias[0], grad_second)


def solution(mesh):
    placed = (
        P("nodes", "feat"),
        P("nodes", None),
        P("nodes", None, None),
        P("nodes", None),
        P("nodes", None, None, None),
        P("nodes"),
        P("feat", None),
        P("feat"),
        P("feat", None),
    )
    return jax.shard_map(
        shards,
        mesh=mesh,
        in_specs=placed,
        out_specs=(P("feat", "nodes"), P("feat"), P("feat", None)),
        check_vma=False,
    )
```

```python
import functools
import math

import jax
import jax.numpy as jnp
from jax import lax
from jax.experimental import pallas as pl
from jax.experimental.pallas import tpu as pltpu
from jax.sharding import PartitionSpec as P

MESH = pl.DeviceIdType.MESH
F32 = jnp.float32
BF16 = jnp.bfloat16


def flip(index, mask):
    bit = 1
    while bit <= mask:
        if mask & bit:
            index = index + bit - 2 * bit * ((index // bit) % 2)
        bit *= 2
    return index


def greet(parts, fsize, me_n, me_f):
    barrier = pltpu.get_barrier_semaphore()
    for d in range(1, fsize):
        pl.semaphore_signal(barrier, inc=1, device_id=(me_n, (me_f + d) % fsize), device_id_type=MESH)
    for d in range(1, parts):
        pl.semaphore_signal(barrier, inc=1, device_id=((me_n + d) % parts, me_f), device_id_type=MESH)
    pl.semaphore_wait(barrier, fsize + parts - 2)


def remote(src, dst, send, recv, device):
    return pltpu.make_async_remote_copy(
        src_ref=src, dst_ref=dst, send_sem=send, recv_sem=recv, device_id=device, device_id_type=MESH
    )


def stage_bits(parts, fsize):
    f_bits = [("f", 1 << i) for i in range(fsize.bit_length() - 1)]
    n_bits = [("n", 1 << i) for i in range(parts.bit_length() - 1)]
    first = f_bits + n_bits
    second = f_bits[:1] + n_bits[:1] + f_bits[1:] + n_bits[1:]
    return (first, second)


def kept(bits, done, fsize, parts):
    gone_f = sum(b for a, b in bits[:done] if a == "f")
    gone_n = sum(b for a, b in bits[:done] if a == "n")
    return [(f, n) for f in range(fsize) for n in range(parts) if not (f & gone_f) and not (n & gone_n)]


def whole_kernel(
    dims, feats_in, w_in, b_in, w2t_in, tiles, src, count, table, labels, grad_out, bias_out, second_out,
    agg, w1, w2, w2_all, b_all, w2t, b1, fsend, frecv_a, frecv_b, abuf,
    part, mask, mask_t, hidden, pall, sbuf, rbuf, r3, tl, dl, contrib, sback, rback, spread, rspread,
    dproj_t, dpre_t, acc, gout, gin, sm, smin, tile_sem,
    w_s, w_r, w2_s, w2_r, b_s, b_r, fx_s, fx_r, tr_s, tr_r,
    ag_s, ag_r, ex_s, ex_r, bk_s, bk_r, sp_s, sp_r, rs_s, rs_r, sm_s, sm_r,
):
    parts, fsize, slots, nblocks, per_block, blk, grades, scale = dims
    me_n, me_f = lax.axis_index("nodes"), lax.axis_index("feat")
    mine = nblocks // fsize
    rows, hid = hidden.shape
    width = rows // 4
    fw = agg.shape[1] // fsize
    hb = hid // parts
    half = fw // 2
    base = me_f * mine

    def live(b, k):
        slot = src[k, b]
        return jnp.where(slot % slots < count[0, slot // slots], 1.0, 0.0)

    fetch = pltpu.make_async_copy(tiles, tl, tile_sem)
    fetch.start()
    frecv = (frecv_a, frecv_b)
    own_w = pl.ds(pl.multiple_of(me_f * fw, fw), fw)
    w1[own_w, :] = w_in[...]
    w2_all[me_f] = w2t_in[...]
    b_all[me_f] = jnp.broadcast_to(b_in[...], (8, fw))
    greet(parts, fsize, me_n, me_f)

    def column(c):
        return slice(c * half, (c + 1) * half)

    def exchange(c, d):
        p = (me_n + d) % parts
        return remote(fsend.at[c, p], frecv[c].at[me_n], fx_s.at[c, d], fx_r.at[c, d], (p, me_f))

    def stage_block(c, p, s):
        fsend[c, p, s] = feats_in[table[s, p], :, column(c)]

    for p in range(parts):
        for s in range(slots):
            stage_block(0, p, s)
    first = []
    for d in range(1, parts):
        x = exchange(0, d)
        x.start()
        first.append(x)

    def pass_on(j, bit, slot):
        at = pl.ds(pl.multiple_of(flip(me_f, j) * fw, fw), fw)
        return remote(w1.at[at, :], w1.at[at, :], w_s.at[slot], w_r.at[slot], (me_n, flip(me_f, bit)))

    weights_flying = []
    far = []
    for j in range(1, fsize):
        if j & (j - 1) == 0:
            x = pass_on(0, j, j)
            x.start()
            (far if j > 1 else weights_flying).append(x)
    for d in range(1, fsize):
        to = (me_n, (me_f + d) % fsize)
        x = remote(w2_all.at[me_f], w2_all.at[me_f], w2_s.at[d], w2_r.at[d], to)
        x.start()
        y = remote(b_all.at[me_f], b_all.at[me_f], b_s.at[d], b_r.at[d], to)
        y.start()
        weights_flying += [x, y]

    for p in range(parts):
        for s in range(slots):
            stage_block(1, p, s)
    frecv_a[me_n] = fsend[0, me_n]
    frecv_b[me_n] = fsend[1, me_n]
    second = []
    for d in range(1, parts):
        first[d - 1].wait_send()
        x = exchange(1, d)
        x.start()
        second.append(x)
    fetch.wait()
    for x in first:
        x.wait_recv()

    order = list(range(fsize - 1, -1, -1))

    def aggregate(c):
        def block(b):
            wcat = jnp.concatenate([tl[b, k] * live(b, k).astype(BF16) for k in range(per_block)], axis=1)
            got = jnp.concatenate(
                [frecv[c][src[k, b] // slots, src[k, b] % slots] for k in range(per_block)], axis=0
            )
            total = jnp.dot(wcat, got, preferred_element_type=F32)
            return (total + feats_in[b, :, column(c)].astype(F32)).astype(BF16)

        lanes = pl.ds(pl.multiple_of(me_f * fw + c * half, half), half)
        sent = []
        for j in order:
            group = flip(me_f, j)

            @pl.loop(0, mine // 4)
            def _(r):
                done = [block(group * mine + r * 4 + i) for i in range(4)]
                for i, got in enumerate(done):
                    if j:
                        to = pl.multiple_of((group * mine + r * 4 + i) * blk, blk)
                        abuf[c, pl.ds(to, blk), :] = got
                    else:
                        agg[pl.ds(pl.multiple_of((r * 4 + i) * blk, blk), blk), lanes] = got

            if j:
                at = pl.ds(pl.multiple_of(group * rows, rows), rows)
                x = remote(abuf.at[c, at, :], agg.at[:, lanes], tr_s.at[c, j], tr_r.at[c, j], (me_n, group))
                x.start()
                sent.append(x)
        return sent

    turned_a = aggregate(0)
    for x in far:
        x.wait()
    for j in range(3, fsize):
        low = j & -j
        if j != low:
            x = pass_on(j - low, low, j)
            x.start()
            weights_flying.append(x)
    for x in second:
        x.wait()
    turned_b = aggregate(1)
    for x in weights_flying:
        x.wait()
    for f in range(fsize):
        b1[:, f * fw : (f + 1) * fw] = b_all[f, :1, :]
        w2t[:, f * fw : (f + 1) * fw] = w2_all[f]
    def depth_half(c, at):
        lhs = jnp.concatenate([agg[at, f * fw + c * half : f * fw + (c + 1) * half] for f in range(fsize)], axis=1)
        rhs = jnp.concatenate([w1[f * fw + c * half : f * fw + (c + 1) * half, :] for f in range(fsize)], axis=0)
        return jnp.dot(lhs, rhs, preferred_element_type=F32)

    for x in turned_a:
        x.wait()

    @pl.loop(0, 4)
    def _(r):
        at = pl.ds(pl.multiple_of(r * width, width), width)
        part[at, :] = depth_half(0, at)

    w2[...] = jnp.concatenate([w2t[...], jnp.zeros((blk - grades, hid), BF16)], axis=0).T
    for x in turned_b:
        x.wait()

    @pl.loop(0, 4)
    def _(r):
        at = pl.ds(pl.multiple_of(r * width, width), width)
        pre = part[at, :] + depth_half(1, at) + b1[...]
        hb16 = jnp.maximum(pre, 0.0).astype(BF16)
        hidden[at, :] = hb16
        mask[at, :] = jnp.where(pre > 0, 1.0, 0.0).astype(BF16)
        pt = lax.dot_general(w2t[...], hb16, (((1,), (1,)), ((), ())), preferred_element_type=F32)
        for i in range(width // blk):
            pall[base + r * (width // blk) + i] = pt[:, i * blk : (i + 1) * blk]

    copies = []
    for d in range(1, fsize):
        own = pall.at[pl.ds(base, mine)]
        c = remote(own, own, ag_s.at[d], ag_r.at[d], (me_n, (me_f + d) % fsize))
        c.start()
        copies.append(c)

    @pl.loop(0, 4)
    def _(r):
        at = pl.ds(pl.multiple_of(r * width, width), width)
        mask_t[:, at] = mask[at, :].T

    for c in copies:
        c.wait()
    for p in range(parts):
        for s in range(slots):
            sbuf[p, s] = pall[table[s, p]]
    rbuf[me_n] = sbuf[me_n]
    copies = []
    for d in range(1, parts):
        p = (me_n + d) % parts
        c = remote(sbuf.at[p], rbuf.at[me_n], ex_s.at[d], ex_r.at[d], (p, me_f))
        c.start()
        copies.append(c)
    for c in copies:
        c.wait()
    for p in range(parts):
        for s in range(slots):
            x = rbuf[p, s]
            hi = x.astype(BF16)
            rest = x - hi.astype(F32)
            mid = rest.astype(BF16)
            low = (rest - mid.astype(F32)).astype(BF16)
            r3[p * slots + s] = jnp.concatenate([hi, mid, low], axis=0)

    grade_id = lax.broadcasted_iota(jnp.int32, (grades, blk), 0)

    @pl.loop(0, mine // 4)
    def _(r):
        four = [r * 4 + i for i in range(4)]
        wcats, outs = [], []
        for b in four:
            pieces = [r3[src[k, base + b]] * live(base + b, k).astype(BF16) for k in range(per_block)]
            lhs = jnp.concatenate(pieces, axis=1)
            wcats.append(jnp.concatenate([tl[base + b, k] for k in range(per_block)], axis=1))
            outs.append(
                lax.dot_general(lhs, wcats[-1], (((1,), (1,)), ((), ())), preferred_element_type=F32)
            )
        dlogs = []
        for b, out in zip(four, outs):
            logits = pall[base + b] + (
                out[:grades] + (out[grades : 2 * grades] + out[2 * grades : 3 * grades])
            )
            expo = jnp.exp(logits)
            probs = expo / jnp.sum(expo, axis=0, keepdims=True)
            onehot = jnp.where(labels[pl.ds(base + b, 1), :] == grade_id, 1.0, 0.0)
            dlogs.append((probs - onehot) * scale)
        backs = [
            jnp.dot(dlog.astype(BF16), wcat, preferred_element_type=F32)
            for dlog, wcat in zip(dlogs, wcats)
        ]
        for b, dlog, back in zip(four, dlogs, backs):
            dl[b] = dlog
            for k in range(per_block):
                contrib[b * per_block + k] = back[:, k * blk : (k + 1) * blk] * live(base + b, k)

    @pl.loop(0, parts)
    def _(p):
        for s in range(slots):
            slot = p * slots + s
            total = jnp.zeros((grades, blk), F32)
            for b in range(mine):
                for k in range(per_block):
                    hit = jnp.where(src[k, base + b] == slot, 1.0, 0.0)
                    total = total + contrib[b * per_block + k] * hit
            sback[p, s] = total.astype(BF16)

    rback[me_n] = sback[me_n]
    copies = []
    for d in range(1, parts):
        p = (me_n + d) % parts
        c = remote(sback.at[p], rback.at[me_n], bk_s.at[d], bk_r.at[d], (p, me_f))
        c.start()
        copies.append(c)
    for c in copies:
        c.wait()

    came = [(rback[p, s].astype(F32), p, s) for p in range(parts) for s in range(slots)]

    @pl.loop(0, nblocks)
    def _(b):
        total = jnp.zeros((grades, blk), F32)
        for x, p, s in came:
            total = total + x * jnp.where(table[s, p] == b, 1.0, 0.0)
        spread[b] = total.astype(BF16)

    copies = []
    for d in range(1, fsize):
        to = (me_f + d) % fsize
        c = remote(
            spread.at[pl.ds(to * mine, mine)], rspread.at[d - 1], sp_s.at[d], sp_r.at[d], (me_n, to)
        )
        c.start()
        copies.append(c)
    for c in copies:
        c.wait()
    for b in range(mine):
        total = spread[base + b].astype(F32)
        for d in range(fsize - 1):
            total = total + rspread[d, b].astype(F32)
        dproj_t[:, b * blk : (b + 1) * blk] = (dl[b] + total).astype(BF16)

    for n in range(parts):
        at = pl.ds(pl.multiple_of(flip(me_n, n) * hb, hb), hb)
        d = jnp.dot(w2[at, :grades], dproj_t[...], preferred_element_type=F32)
        dpre_t[n * hb : (n + 1) * hb, :] = jnp.where(mask_t[at, :] > 0, d, 0.0).astype(BF16)

    orders = stage_bits(parts, fsize)
    stages = len(orders[0])
    sizes = [(fsize * parts) >> (t + 1) for t in range(stages)]
    starts = [sum(sizes[:t]) for t in range(stages)]

    def product(f):
        at = pl.ds(pl.multiple_of(flip(me_f, f) * fw, fw), fw)
        return jnp.dot(dpre_t[...], agg[:, at], preferred_element_type=F32)

    def partner(axis, bit):
        return (flip(me_n, bit), me_f) if axis == "n" else (me_n, flip(me_f, bit))

    def launch(c, t):
        at = pl.ds(starts[t], sizes[t])
        r = remote(gout.at[c, at], gin.at[c, at], rs_s.at[c, t], rs_r.at[c, t], partner(*orders[c][t]))
        r.start()
        return r

    def going(c, t):
        axis, bit = orders[c][t]
        return [j for j in kept(orders[c], t, fsize, parts) if (j[0] if axis == "f" else j[1]) & bit]

    flying = [None, None]
    for f in range(fsize):
        if f & 1:
            g = product(f).astype(BF16)
            for c in range(2):
                for i, j in enumerate(going(c, 0)):
                    if j[0] == f:
                        gout[c, i] = g[j[1] * hb : (j[1] + 1) * hb, c * half : (c + 1) * half]
    for c in range(2):
        flying[c] = launch(c, 0)
    for f in range(fsize):
        if not f & 1:
            g = product(f)
            for c in range(2):
                for n in range(parts):
                    acc[c, f, n] = g[n * hb : (n + 1) * hb, c * half : (c + 1) * half]

    both = jnp.dot(dproj_t[...], hidden[...], preferred_element_type=F32)
    bias = jnp.sum(
        w2t[...].astype(F32) * jnp.dot(dproj_t[...], mask[...], preferred_element_type=F32),
        axis=0,
        keepdims=True,
    )
    small_full = jnp.concatenate([both, jnp.broadcast_to(bias, (8, hid))], axis=0)
    rel = [small_full[:, g * fw : (g + 1) * fw] for g in range(fsize)]
    for f in range(fsize):
        pick = flip(me_f, f)
        total = rel[0]
        for g in range(1, fsize):
            total = jnp.where(pick == g, rel[g], total)
        sm[f] = total

    small_bits = orders[0]
    at_small = 0
    for t in range(stages):
        axis, bit = small_bits[t]
        if axis == "f":
            idx = [f for f in range(fsize) if not f & (bit - 1) and f & bit]
        else:
            idx = [0]
        smalls = []
        for f in idx:
            r = remote(sm.at[f], smin.at[at_small], sm_s.at[at_small], sm_r.at[at_small], partner(axis, bit))
            r.start()
            smalls.append((f - bit if axis == "f" else 0, at_small, r))
            at_small += 1
        for c in range(2):
            flying[c].wait()
            sent = going(c, t)
            axis_c, bit_c = orders[c][t]
            for i, j in enumerate(sent):
                k = (j[0] - bit_c, j[1]) if axis_c == "f" else (j[0], j[1] - bit_c)
                new = acc[c, k[0], k[1]] + gin[c, starts[t] + i].astype(F32)
                nxt = going(c, t + 1) if t + 1 < stages else []
                if k in nxt:
                    gout[c, starts[t + 1] + nxt.index(k)] = new.astype(BF16)
                elif t + 1 < stages:
                    acc[c, k[0], k[1]] = new
                else:
                    grad_out[c * half : (c + 1) * half, :] = new.T
            if t + 1 < stages:
                flying[c] = launch(c, t + 1)
        for _, _, r in smalls:
            r.wait()
        for f, slot, _ in smalls:
            sm[f] = sm[f] + smin[slot]
    bias_out[...] = sm[0, grades : grades + 1, :]
    second_out[...] = sm[0, :grades, :]


def shards(features, pair_count, send_blocks, tile_src, tiles, labels, w_first, b_first, w_second):
    nodes, fw = features.shape
    nblocks, per_block = tile_src.shape
    blk = tiles.shape[2]
    parts = lax.axis_size("nodes")
    fsize = lax.axis_size("feat")
    slots = send_blocks.shape[2]
    grades = w_second.shape[1]
    mine = nblocks // fsize
    rows, feats, hid = nodes // fsize, fw * fsize, w_first.shape[1]
    hb = hid // parts
    half = fw // 2
    dims = (parts, fsize, slots, nblocks, per_block, blk, grades, 1.0 / math.sqrt(nodes * parts))
    stages = len(stage_bits(parts, fsize)[0])
    tiles_sent = fsize * parts - 1
    n_small = (fsize - 1) + (parts.bit_length() - 1)
    vm = pl.BlockSpec(memory_space=pltpu.VMEM)
    sc = pl.BlockSpec(memory_space=pltpu.SMEM)
    dma = pltpu.SemaphoreType.DMA
    field = (grades, blk)
    grad_first, grad_bias, grad_second = pl.pallas_call(
        functools.partial(whole_kernel, dims),
        out_shape=(
            jax.ShapeDtypeStruct((fw, hb), F32),
            jax.ShapeDtypeStruct((1, fw), F32),
            jax.ShapeDtypeStruct((grades, fw), F32),
        ),
        in_specs=[vm, vm, vm, vm, pl.BlockSpec(memory_space=pl.ANY), sc, sc, sc, vm],
        out_specs=(vm, vm, vm),
        scratch_shapes=[
            pltpu.VMEM((rows, feats), BF16),
            pltpu.VMEM((feats, hid), BF16),
            pltpu.VMEM((hid, blk), BF16),
            pltpu.VMEM((fsize, grades, fw), BF16),
            pltpu.VMEM((fsize, 8, fw), F32),
            pltpu.VMEM((grades, hid), BF16),
            pltpu.VMEM((1, hid), F32),
            pltpu.VMEM((2, parts, slots, blk, half), BF16),
            pltpu.VMEM((parts, slots, blk, half), BF16),
            pltpu.VMEM((parts, slots, blk, half), BF16),
            pltpu.VMEM((2, nodes, half), BF16),
            pltpu.VMEM((rows, hid), F32),
            pltpu.VMEM((rows, hid), BF16),
            pltpu.VMEM((hid, rows), BF16),
            pltpu.VMEM((rows, hid), BF16),
            pltpu.VMEM((nblocks,) + field, F32),
            pltpu.VMEM((parts, slots) + field, F32),
            pltpu.VMEM((parts, slots) + field, F32),
            pltpu.VMEM((parts * slots, 3 * grades, blk), BF16),
            pltpu.VMEM((nblocks, per_block, blk, blk), BF16),
            pltpu.VMEM((mine,) + field, F32),
            pltpu.VMEM((mine * per_block,) + field, F32),
            pltpu.VMEM((parts, slots) + field, BF16),
            pltpu.VMEM((parts, slots) + field, BF16),
            pltpu.VMEM((nblocks,) + field, BF16),
            pltpu.VMEM((fsize - 1, mine) + field, BF16),
            pltpu.VMEM((grades, rows), BF16),
            pltpu.VMEM((hid, rows), BF16),
            pltpu.VMEM((2, fsize, parts, hb, half), F32),
            pltpu.VMEM((2, tiles_sent, hb, half), BF16),
            pltpu.VMEM((2, tiles_sent, hb, half), BF16),
            pltpu.VMEM((fsize, grades + 8, fw), F32),
            pltpu.VMEM((n_small, grades + 8, fw), F32),
            dma,
            dma((fsize,)), dma((fsize,)),
            dma((fsize,)), dma((fsize,)),
            dma((fsize,)), dma((fsize,)),
            dma((2, parts)), dma((2, parts)),
            dma((2, fsize)), dma((2, fsize)),
            dma((fsize,)), dma((fsize,)),
            dma((parts,)), dma((parts,)),
            dma((parts,)), dma((parts,)),
            dma((fsize,)), dma((fsize,)),
            dma((2, stages)), dma((2, stages)),
            dma((n_small,)), dma((n_small,)),
        ],
        compiler_params=pltpu.CompilerParams(
            collective_id=1, has_side_effects=True, vmem_limit_bytes=60 * 1024 * 1024
        ),
        cost_estimate=pl.CostEstimate(
            flops=4 * rows * hid * feats, bytes_accessed=6 * rows * hid, transcendentals=rows * grades
        ),
    )(
        features.reshape(nblocks, blk, fw), w_first, b_first[None, :], w_second.T, tiles, tile_src.T,
        pair_count, send_blocks[0].T, labels.reshape(nblocks, blk),
    )
    return (grad_first, grad_bias[0], grad_second.T)


def solution(mesh):
    placed = (
        P("nodes", "feat"),
        P("nodes", None),
        P("nodes", None, None),
        P("nodes", None),
        P("nodes", None, None, None),
        P("nodes"),
        P("feat", None),
        P("feat"),
        P("feat", None),
    )
    return jax.shard_map(
        shards,
        mesh=mesh,
        in_specs=placed,
        out_specs=(P("feat", "nodes"), P("feat"), P("feat", None)),
        check_vma=False,
    )
```

```python
import functools
import math

import jax
import jax.numpy as jnp
from jax import lax
from jax.experimental import pallas as pl
from jax.experimental.pallas import tpu as pltpu
from jax.sharding import PartitionSpec as P

MESH = pl.DeviceIdType.MESH
F32 = jnp.float32
BF16 = jnp.bfloat16


def flip(index, mask):
    bit = 1
    while bit <= mask:
        if mask & bit:
            index = index + bit - 2 * bit * ((index // bit) % 2)
        bit *= 2
    return index


def greet(parts, fsize, me_n, me_f):
    barrier = pltpu.get_barrier_semaphore()
    for d in range(1, fsize):
        pl.semaphore_signal(barrier, inc=1, device_id=(me_n, (me_f + d) % fsize), device_id_type=MESH)
    for d in range(1, parts):
        pl.semaphore_signal(barrier, inc=1, device_id=((me_n + d) % parts, me_f), device_id_type=MESH)
    return barrier


def remote(src, dst, send, recv, device):
    return pltpu.make_async_remote_copy(
        src_ref=src, dst_ref=dst, send_sem=send, recv_sem=recv, device_id=device, device_id_type=MESH
    )


def stage_bits(parts, fsize):
    f_bits = [("f", 1 << i) for i in range(fsize.bit_length() - 1)]
    n_bits = [("n", 1 << i) for i in range(parts.bit_length() - 1)]
    first = f_bits + n_bits
    second = f_bits[:1] + n_bits[:1] + f_bits[1:] + n_bits[1:]
    return (first, second)


def kept(bits, done, fsize, parts):
    gone_f = sum(b for a, b in bits[:done] if a == "f")
    gone_n = sum(b for a, b in bits[:done] if a == "n")
    return [(f, n) for f in range(fsize) for n in range(parts) if not (f & gone_f) and not (n & gone_n)]


def whole_kernel(
    dims, feats_hbm, w_hbm, b_in, w2t_in, tiles, src, count, table, labels, grad_out, bias_out, second_out,
    feats_in, agg, w1, w2, w2_all, b_all, w2t, b1, fsend, frecv_a, frecv_b, abuf,
    part, mask, mask_t, hidden, pall, sbuf, rbuf, r3, tl, dl, contrib, sback, rback, spread, rspread,
    dproj_t, dpre_t, acc, gout, gin, sm, smin, tile_sem, feat_sem, w_sem,
    w_s, w_r, w2_s, w2_r, b_s, b_r, fx_s, fx_r, tr_s, tr_r,
    ag_s, ag_r, ex_s, ex_r, bk_s, bk_r, sp_s, sp_r, z_s, z_r, rs_s, rs_r, sm_s, sm_r,
):
    parts, fsize, slots, nblocks, per_block, blk, grades, scale = dims
    me_n, me_f = lax.axis_index("nodes"), lax.axis_index("feat")
    mine = nblocks // fsize
    rows, hid = hidden.shape
    width = rows // 4
    fw = agg.shape[1] // fsize
    hb = hid // parts
    half = fw // 2
    base = me_f * mine

    def live(b, k):
        slot = src[k, b]
        return jnp.where(slot % slots < count[0, slot // slots], 1.0, 0.0)

    barrier = greet(parts, fsize, me_n, me_f)
    frecv = (frecv_a, frecv_b)
    own_w = pl.ds(pl.multiple_of(me_f * fw, fw), fw)
    fetch_feats = pltpu.make_async_copy(feats_hbm, feats_in, feat_sem)
    fetch_feats.start()
    fetch_w = pltpu.make_async_copy(w_hbm, w1.at[own_w, :], w_sem)
    fetch_w.start()
    fetch = pltpu.make_async_copy(tiles, tl, tile_sem)
    fetch.start()
    w2_all[me_f] = w2t_in[...]
    b_all[me_f] = jnp.broadcast_to(b_in[...], (8, fw))

    def column(c):
        return slice(c * half, (c + 1) * half)

    def exchange(c, d):
        p = (me_n + d) % parts
        return remote(fsend.at[c, p], frecv[c].at[me_n], fx_s.at[c, d], fx_r.at[c, d], (p, me_f))

    def stage_block(c, p, s):
        fsend[c, p, s] = feats_in[table[s, p], :, column(c)]

    fetch_feats.wait()
    for p in range(parts):
        for s in range(slots):
            stage_block(0, p, s)
    pl.semaphore_wait(barrier, fsize + parts - 2)
    first = []
    for d in range(1, parts):
        x = exchange(0, d)
        x.start()
        first.append(x)

    def pass_on(j, bit, slot):
        at = pl.ds(pl.multiple_of(flip(me_f, j) * fw, fw), fw)
        return remote(w1.at[at, :], w1.at[at, :], w_s.at[slot], w_r.at[slot], (me_n, flip(me_f, bit)))

    weights_flying = []
    far = []
    fetch_w.wait()
    for j in range(1, fsize):
        if j & (j - 1) == 0:
            x = pass_on(0, j, j)
            x.start()
            (far if j > 1 else weights_flying).append(x)
    for d in range(1, fsize):
        to = (me_n, (me_f + d) % fsize)
        x = remote(w2_all.at[me_f], w2_all.at[me_f], w2_s.at[d], w2_r.at[d], to)
        x.start()
        y = remote(b_all.at[me_f], b_all.at[me_f], b_s.at[d], b_r.at[d], to)
        y.start()
        weights_flying += [x, y]

    for p in range(parts):
        for s in range(slots):
            stage_block(1, p, s)
    frecv_a[me_n] = fsend[0, me_n]
    frecv_b[me_n] = fsend[1, me_n]
    second = []
    for d in range(1, parts):
        first[d - 1].wait_send()
        x = exchange(1, d)
        x.start()
        second.append(x)
    fetch.wait()
    for x in first:
        x.wait_recv()

    order = list(range(fsize - 1, -1, -1))

    def aggregate(c):
        def block(b):
            wcat = jnp.concatenate([tl[b, k] * live(b, k).astype(BF16) for k in range(per_block)], axis=1)
            got = jnp.concatenate(
                [frecv[c][src[k, b] // slots, src[k, b] % slots] for k in range(per_block)], axis=0
            )
            total = jnp.dot(wcat, got, preferred_element_type=F32)
            return (total + feats_in[b, :, column(c)].astype(F32)).astype(BF16)

        lanes = pl.ds(pl.multiple_of(me_f * fw + c * half, half), half)
        sent = []
        for j in order:
            group = flip(me_f, j)

            @pl.loop(0, mine // 4)
            def _(r):
                done = [block(group * mine + r * 4 + i) for i in range(4)]
                for i, got in enumerate(done):
                    if j:
                        to = pl.multiple_of((group * mine + r * 4 + i) * blk, blk)
                        abuf[c, pl.ds(to, blk), :] = got
                    else:
                        agg[pl.ds(pl.multiple_of((r * 4 + i) * blk, blk), blk), lanes] = got

            if j:
                at = pl.ds(pl.multiple_of(group * rows, rows), rows)
                x = remote(abuf.at[c, at, :], agg.at[:, lanes], tr_s.at[c, j], tr_r.at[c, j], (me_n, group))
                x.start()
                sent.append(x)
        return sent

    turned_a = aggregate(0)
    for x in far:
        x.wait()
    for j in range(3, fsize):
        low = j & -j
        if j != low:
            x = pass_on(j - low, low, j)
            x.start()
            weights_flying.append(x)
    for x in second:
        x.wait()
    turned_b = aggregate(1)
    for x in weights_flying:
        x.wait()
    for f in range(fsize):
        b1[:, f * fw : (f + 1) * fw] = b_all[f, :1, :]
        w2t[:, f * fw : (f + 1) * fw] = w2_all[f]
    def depth_half(c, at):
        lhs = jnp.concatenate([agg[at, f * fw + c * half : f * fw + (c + 1) * half] for f in range(fsize)], axis=1)
        rhs = jnp.concatenate([w1[f * fw + c * half : f * fw + (c + 1) * half, :] for f in range(fsize)], axis=0)
        return jnp.dot(lhs, rhs, preferred_element_type=F32)

    for x in turned_a:
        x.wait()

    @pl.loop(0, 4)
    def _(r):
        at = pl.ds(pl.multiple_of(r * width, width), width)
        part[at, :] = depth_half(0, at)

    w2[...] = jnp.concatenate([w2t[...], jnp.zeros((blk - grades, hid), BF16)], axis=0).T
    for x in turned_b:
        x.wait()

    copies = []
    per = width // blk
    for r in range(4):
        at = slice(r * width, (r + 1) * width)
        pre = part[at, :] + depth_half(1, at) + b1[...]
        hb16 = jnp.maximum(pre, 0.0).astype(BF16)
        hidden[at, :] = hb16
        mask[at, :] = jnp.where(pre > 0, 1.0, 0.0).astype(BF16)
        pt = lax.dot_general(w2t[...], hb16, (((1,), (1,)), ((), ())), preferred_element_type=F32)
        for i in range(per):
            pall[base + r * per + i] = pt[:, i * blk : (i + 1) * blk]
        for d in range(1, fsize):
            own = pall.at[pl.ds(base + r * per, per)]
            c = remote(own, own, ag_s.at[r, d], ag_r.at[r, d], (me_n, (me_f + d) % fsize))
            c.start()
            copies.append(c)

    @pl.loop(0, 4)
    def _(r):
        at = pl.ds(pl.multiple_of(r * width, width), width)
        mask_t[:, at] = mask[at, :].T

    for c in copies:
        c.wait()
    for p in range(parts):
        for s in range(slots):
            sbuf[p, s] = pall[table[s, p]]
    rbuf[me_n] = sbuf[me_n]
    copies = []
    for d in range(1, parts):
        p = (me_n + d) % parts
        c = remote(sbuf.at[p], rbuf.at[me_n], ex_s.at[d], ex_r.at[d], (p, me_f))
        c.start()
        copies.append(c)
    for c in copies:
        c.wait()
    for p in range(parts):
        for s in range(slots):
            x = rbuf[p, s]
            hi = x.astype(BF16)
            rest = x - hi.astype(F32)
            mid = rest.astype(BF16)
            low = (rest - mid.astype(F32)).astype(BF16)
            r3[p * slots + s] = jnp.concatenate([hi, mid, low], axis=0)

    grade_id = lax.broadcasted_iota(jnp.int32, (grades, blk), 0)

    @pl.loop(0, mine // 4)
    def _(r):
        four = [r * 4 + i for i in range(4)]
        wcats, outs = [], []
        for b in four:
            pieces = [r3[src[k, base + b]] * live(base + b, k).astype(BF16) for k in range(per_block)]
            lhs = jnp.concatenate(pieces, axis=1)
            wcats.append(jnp.concatenate([tl[base + b, k] for k in range(per_block)], axis=1))
            outs.append(
                lax.dot_general(lhs, wcats[-1], (((1,), (1,)), ((), ())), preferred_element_type=F32)
            )
        dlogs = []
        for b, out in zip(four, outs):
            logits = pall[base + b] + (
                out[:grades] + (out[grades : 2 * grades] + out[2 * grades : 3 * grades])
            )
            expo = jnp.exp(logits)
            probs = expo / jnp.sum(expo, axis=0, keepdims=True)
            onehot = jnp.where(labels[pl.ds(base + b, 1), :] == grade_id, 1.0, 0.0)
            dlogs.append((probs - onehot) * scale)
        backs = [
            jnp.dot(dlog.astype(BF16), wcat, preferred_element_type=F32)
            for dlog, wcat in zip(dlogs, wcats)
        ]
        for b, dlog, back in zip(four, dlogs, backs):
            dl[b] = dlog
            for k in range(per_block):
                contrib[b * per_block + k] = back[:, k * blk : (k + 1) * blk] * live(base + b, k)

    @pl.loop(0, parts)
    def _(p):
        for s in range(slots):
            slot = p * slots + s
            total = jnp.zeros((grades, blk), F32)
            for b in range(mine):
                for k in range(per_block):
                    hit = jnp.where(src[k, base + b] == slot, 1.0, 0.0)
                    total = total + contrib[b * per_block + k] * hit
            sback[p, s] = total.astype(BF16)

    rback[me_n] = sback[me_n]
    copies = []
    for d in range(1, parts):
        p = (me_n + d) % parts
        c = remote(sback.at[p], rback.at[me_n], bk_s.at[d], bk_r.at[d], (p, me_f))
        c.start()
        copies.append(c)
    for c in copies:
        c.wait()

    came = [(rback[p, s].astype(F32), p, s) for p in range(parts) for s in range(slots)]

    @pl.loop(0, nblocks)
    def _(b):
        total = jnp.zeros((grades, blk), F32)
        for x, p, s in came:
            total = total + x * jnp.where(table[s, p] == b, 1.0, 0.0)
        spread[b] = total.astype(BF16)

    copies = []
    for d in range(1, fsize):
        to = (me_f + d) % fsize
        c = remote(
            spread.at[pl.ds(to * mine, mine)], rspread.at[d - 1], sp_s.at[d], sp_r.at[d], (me_n, to)
        )
        c.start()
        copies.append(c)
    for c in copies:
        c.wait()
    for b in range(mine):
        total = spread[base + b].astype(F32)
        for d in range(fsize - 1):
            total = total + rspread[d, b].astype(F32)
        dproj_t[:, b * blk : (b + 1) * blk] = (dl[b] + total).astype(BF16)

    for n in range(parts):
        at = pl.ds(pl.multiple_of(flip(me_n, n) * hb, hb), hb)
        d = jnp.dot(w2[at, :grades], dproj_t[...], preferred_element_type=F32)
        dpre_t[n * hb : (n + 1) * hb, :] = jnp.where(mask_t[at, :] > 0, d, 0.0).astype(BF16)

    orders = stage_bits(parts, fsize)
    stages = len(orders[0])
    sizes = [(fsize * parts) >> (t + 1) for t in range(stages)]
    starts = [sum(sizes[:t]) for t in range(stages)]

    def product(f):
        at = pl.ds(pl.multiple_of(flip(me_f, f) * fw, fw), fw)
        return jnp.dot(dpre_t[...], agg[:, at], preferred_element_type=F32)

    def partner(axis, bit):
        return (flip(me_n, bit), me_f) if axis == "n" else (me_n, flip(me_f, bit))

    def launch(c, t):
        at = pl.ds(starts[t], sizes[t])
        r = remote(gout.at[c, at], gin.at[c, at], rs_s.at[c, t], rs_r.at[c, t], partner(*orders[c][t]))
        r.start()
        return r

    def going(c, t):
        axis, bit = orders[c][t]
        return [j for j in kept(orders[c], t, fsize, parts) if (j[0] if axis == "f" else j[1]) & bit]

    flying = [[], []]
    for f in range(fsize - 1, 0, -2):
        g = product(f).astype(BF16)
        for c in range(2):
            first_tile = (f // 2) * parts
            for n in range(parts):
                gout[c, first_tile + n] = g[n * hb : (n + 1) * hb, c * half : (c + 1) * half]
            at = pl.ds(first_tile, parts)
            r = remote(gout.at[c, at], gin.at[c, at], z_s.at[c, f], z_r.at[c, f], partner("f", 1))
            r.start()
            flying[c].append(r)
    for f in range(fsize):
        if not f & 1:
            g = product(f)
            for c in range(2):
                for n in range(parts):
                    acc[c, f, n] = g[n * hb : (n + 1) * hb, c * half : (c + 1) * half]

    both = jnp.dot(dproj_t[...], hidden[...], preferred_element_type=F32)
    bias = jnp.sum(
        w2t[...].astype(F32) * jnp.dot(dproj_t[...], mask[...], preferred_element_type=F32),
        axis=0,
        keepdims=True,
    )
    small_full = jnp.concatenate([both, jnp.broadcast_to(bias, (8, hid))], axis=0)
    rel = [small_full[:, g * fw : (g + 1) * fw] for g in range(fsize)]
    for f in range(fsize):
        pick = flip(me_f, f)
        total = rel[0]
        for g in range(1, fsize):
            total = jnp.where(pick == g, rel[g], total)
        sm[f] = total

    small_bits = orders[0]
    at_small = 0
    for t in range(stages):
        axis, bit = small_bits[t]
        if axis == "f":
            idx = [f for f in range(fsize) if not f & (bit - 1) and f & bit]
        else:
            idx = [0]
        smalls = []
        for f in idx:
            r = remote(sm.at[f], smin.at[at_small], sm_s.at[at_small], sm_r.at[at_small], partner(axis, bit))
            r.start()
            smalls.append((f - bit if axis == "f" else 0, at_small, r))
            at_small += 1
        for c in range(2):
            for r in flying[c]:
                r.wait()
            sent = going(c, t)
            axis_c, bit_c = orders[c][t]
            for i, j in enumerate(sent):
                k = (j[0] - bit_c, j[1]) if axis_c == "f" else (j[0], j[1] - bit_c)
                new = acc[c, k[0], k[1]] + gin[c, starts[t] + i].astype(F32)
                nxt = going(c, t + 1) if t + 1 < stages else []
                if k in nxt:
                    gout[c, starts[t + 1] + nxt.index(k)] = new.astype(BF16)
                elif t + 1 < stages:
                    acc[c, k[0], k[1]] = new
                else:
                    grad_out[c * half : (c + 1) * half, :] = new.T
            if t + 1 < stages:
                flying[c] = [launch(c, t + 1)]
        for _, _, r in smalls:
            r.wait()
        for f, slot, _ in smalls:
            sm[f] = sm[f] + smin[slot]
    bias_out[...] = sm[0, grades : grades + 1, :]
    second_out[...] = sm[0, :grades, :]


def hand_over(a, b, c, a_out, b_out, c_out):
    a_out[...] = a[...]
    b_out[...] = b[...]
    c_out[...] = c[...]


def shards(features, pair_count, send_blocks, tile_src, tiles, labels, w_first, b_first, w_second):
    nodes, fw = features.shape
    nblocks, per_block = tile_src.shape
    blk = tiles.shape[2]
    parts = lax.axis_size("nodes")
    fsize = lax.axis_size("feat")
    slots = send_blocks.shape[2]
    grades = w_second.shape[1]
    mine = nblocks // fsize
    rows, feats, hid = nodes // fsize, fw * fsize, w_first.shape[1]
    hb = hid // parts
    half = fw // 2
    dims = (parts, fsize, slots, nblocks, per_block, blk, grades, 1.0 / math.sqrt(nodes * parts))
    stages = len(stage_bits(parts, fsize)[0])
    tiles_sent = fsize * parts - 1
    n_small = (fsize - 1) + (parts.bit_length() - 1)
    vm = pl.BlockSpec(memory_space=pltpu.VMEM)
    sc = pl.BlockSpec(memory_space=pltpu.SMEM)
    hbm = pl.BlockSpec(memory_space=pl.ANY)
    dma = pltpu.SemaphoreType.DMA
    field = (grades, blk)
    grad_first, grad_bias, grad_second = pl.pallas_call(
        functools.partial(whole_kernel, dims),
        out_shape=(
            jax.ShapeDtypeStruct((fw, hb), F32),
            jax.ShapeDtypeStruct((1, fw), F32),
            jax.ShapeDtypeStruct((grades, fw), F32),
        ),
        in_specs=[hbm, hbm, vm, vm, hbm, sc, sc, sc, vm],
        out_specs=(vm, vm, vm),
        scratch_shapes=[
            pltpu.VMEM((nblocks, blk, fw), BF16),
            pltpu.VMEM((rows, feats), BF16),
            pltpu.VMEM((feats, hid), BF16),
            pltpu.VMEM((hid, blk), BF16),
            pltpu.VMEM((fsize, grades, fw), BF16),
            pltpu.VMEM((fsize, 8, fw), F32),
            pltpu.VMEM((grades, hid), BF16),
            pltpu.VMEM((1, hid), F32),
            pltpu.VMEM((2, parts, slots, blk, half), BF16),
            pltpu.VMEM((parts, slots, blk, half), BF16),
            pltpu.VMEM((parts, slots, blk, half), BF16),
            pltpu.VMEM((2, nodes, half), BF16),
            pltpu.VMEM((rows, hid), F32),
            pltpu.VMEM((rows, hid), BF16),
            pltpu.VMEM((hid, rows), BF16),
            pltpu.VMEM((rows, hid), BF16),
            pltpu.VMEM((nblocks,) + field, F32),
            pltpu.VMEM((parts, slots) + field, F32),
            pltpu.VMEM((parts, slots) + field, F32),
            pltpu.VMEM((parts * slots, 3 * grades, blk), BF16),
            pltpu.VMEM((nblocks, per_block, blk, blk), BF16),
            pltpu.VMEM((mine,) + field, F32),
            pltpu.VMEM((mine * per_block,) + field, F32),
            pltpu.VMEM((parts, slots) + field, BF16),
            pltpu.VMEM((parts, slots) + field, BF16),
            pltpu.VMEM((nblocks,) + field, BF16),
            pltpu.VMEM((fsize - 1, mine) + field, BF16),
            pltpu.VMEM((grades, rows), BF16),
            pltpu.VMEM((hid, rows), BF16),
            pltpu.VMEM((2, fsize, parts, hb, half), F32),
            pltpu.VMEM((2, tiles_sent, hb, half), BF16),
            pltpu.VMEM((2, tiles_sent, hb, half), BF16),
            pltpu.VMEM((fsize, grades + 8, fw), F32),
            pltpu.VMEM((n_small, grades + 8, fw), F32),
            dma,
            dma,
            dma,
            dma((fsize,)), dma((fsize,)),
            dma((fsize,)), dma((fsize,)),
            dma((fsize,)), dma((fsize,)),
            dma((2, parts)), dma((2, parts)),
            dma((2, fsize)), dma((2, fsize)),
            dma((4, fsize)), dma((4, fsize)),
            dma((parts,)), dma((parts,)),
            dma((parts,)), dma((parts,)),
            dma((fsize,)), dma((fsize,)),
            dma((2, fsize)), dma((2, fsize)),
            dma((2, stages)), dma((2, stages)),
            dma((n_small,)), dma((n_small,)),
        ],
        compiler_params=pltpu.CompilerParams(
            collective_id=1, has_side_effects=True, vmem_limit_bytes=60 * 1024 * 1024
        ),
        cost_estimate=pl.CostEstimate(
            flops=4 * rows * hid * feats, bytes_accessed=6 * rows * hid, transcendentals=rows * grades
        ),
    )(
        features.reshape(nblocks, blk, fw), w_first, b_first[None, :], w_second.T, tiles, tile_src.T,
        pair_count, send_blocks[0].T, labels.reshape(nblocks, blk),
    )
    grad_first, grad_bias, grad_second = pl.pallas_call(
        hand_over,
        out_shape=tuple(jax.ShapeDtypeStruct(x.shape, F32) for x in (grad_first, grad_bias, grad_second)),
        in_specs=[vm, vm, vm],
        out_specs=(vm, vm, vm),
    )(grad_first, grad_bias, grad_second)
    return (grad_first, grad_bias[0], grad_second.T)


def solution(mesh):
    placed = (
        P("nodes", "feat"),
        P("nodes", None),
        P("nodes", None, None),
        P("nodes", None),
        P("nodes", None, None, None),
        P("nodes"),
        P("feat", None),
        P("feat"),
        P("feat", None),
    )
    return jax.shard_map(
        shards,
        mesh=mesh,
        in_specs=placed,
        out_specs=(P("feat", "nodes"), P("feat"), P("feat", None)),
        check_vma=False,
    )
```

```python
import functools
import math

import jax
import jax.numpy as jnp
from jax import lax
from jax.experimental import pallas as pl
from jax.experimental.pallas import tpu as pltpu
from jax.sharding import PartitionSpec as P

MESH = pl.DeviceIdType.MESH
F32 = jnp.float32
BF16 = jnp.bfloat16


def flip(index, mask):
    bit = 1
    while bit <= mask:
        if mask & bit:
            index = index + bit - 2 * bit * ((index // bit) % 2)
        bit *= 2
    return index


def greet(parts, fsize, me_n, me_f):
    barrier = pltpu.get_barrier_semaphore()
    for d in range(1, fsize):
        pl.semaphore_signal(barrier, inc=1, device_id=(me_n, (me_f + d) % fsize), device_id_type=MESH)
    for d in range(1, parts):
        pl.semaphore_signal(barrier, inc=1, device_id=((me_n + d) % parts, me_f), device_id_type=MESH)
    return barrier


def remote(src, dst, send, recv, device):
    return pltpu.make_async_remote_copy(
        src_ref=src, dst_ref=dst, send_sem=send, recv_sem=recv, device_id=device, device_id_type=MESH
    )


def stage_bits(parts, fsize):
    f_bits = [("f", 1 << i) for i in range(fsize.bit_length() - 1)]
    n_bits = [("n", 1 << i) for i in range(parts.bit_length() - 1)]
    first = f_bits + n_bits
    second = f_bits[:1] + n_bits[:1] + f_bits[1:] + n_bits[1:]
    return (first, second)


def kept(bits, done, fsize, parts):
    gone_f = sum(b for a, b in bits[:done] if a == "f")
    gone_n = sum(b for a, b in bits[:done] if a == "n")
    return [(f, n) for f in range(fsize) for n in range(parts) if not (f & gone_f) and not (n & gone_n)]


def whole_kernel(
    dims, feats_hbm, w_hbm, b_in, w2t_in, tiles, src, count, table, labels, grad_out, bias_out, second_out,
    feats_in, agg, w1, w2, w2_all, b_all, w2t, b1, fsend, frecv_a, frecv_b, abuf,
    part, mask, mask_t, hidden, pall, sbuf, rbuf, r3, tl, dl, contrib, sback, rback, spread, rspread,
    dproj_t, dpre_t, acc, gout, gin, sm, smin, tile_sem, feat_sem, w_sem,
    w_s, w_r, w2_s, w2_r, b_s, b_r, fx_s, fx_r, tr_s, tr_r,
    ag_s, ag_r, ex_s, ex_r, bk_s, bk_r, sp_s, sp_r, z_s, z_r, rs_s, rs_r, sm_s, sm_r,
):
    parts, fsize, slots, nblocks, per_block, blk, grades, scale = dims
    me_n, me_f = lax.axis_index("nodes"), lax.axis_index("feat")
    mine = nblocks // fsize
    rows, hid = hidden.shape
    width = rows // 4
    fw = agg.shape[1] // fsize
    hb = hid // parts
    half = fw // 2
    base = me_f * mine

    def live(b, k):
        slot = src[k, b]
        return jnp.where(slot % slots < count[0, slot // slots], 1.0, 0.0)

    barrier = greet(parts, fsize, me_n, me_f)
    frecv = (frecv_a, frecv_b)
    own_w = pl.ds(pl.multiple_of(me_f * fw, fw), fw)
    fetch_feats = pltpu.make_async_copy(feats_hbm, feats_in, feat_sem)
    fetch_feats.start()
    fetch_w = pltpu.make_async_copy(w_hbm, w1.at[own_w, :], w_sem)
    fetch_w.start()
    fetch = pltpu.make_async_copy(tiles, tl, tile_sem)
    fetch.start()
    w2_all[me_f] = w2t_in[...]
    b_all[me_f] = jnp.broadcast_to(b_in[...], (8, fw))

    def column(c):
        return slice(c * half, (c + 1) * half)

    def exchange(c, d):
        p = (me_n + d) % parts
        return remote(fsend.at[c, p], frecv[c].at[me_n], fx_s.at[c, d], fx_r.at[c, d], (p, me_f))

    def stage_block(c, p, s):
        fsend[c, p, s] = feats_in[table[s, p], :, column(c)]

    fetch_feats.wait()
    for p in range(parts):
        for s in range(slots):
            stage_block(0, p, s)
    pl.semaphore_wait(barrier, fsize + parts - 2)
    first = []
    for d in range(1, parts):
        x = exchange(0, d)
        x.start()
        first.append(x)

    def pass_on(j, bit, slot):
        at = pl.ds(pl.multiple_of(flip(me_f, j) * fw, fw), fw)
        return remote(w1.at[at, :], w1.at[at, :], w_s.at[slot], w_r.at[slot], (me_n, flip(me_f, bit)))

    weights_flying = []
    far = []
    fetch_w.wait()
    for j in range(1, fsize):
        if j & (j - 1) == 0:
            x = pass_on(0, j, j)
            x.start()
            (far if j > 1 else weights_flying).append(x)
    for d in range(1, fsize):
        to = (me_n, (me_f + d) % fsize)
        x = remote(w2_all.at[me_f], w2_all.at[me_f], w2_s.at[d], w2_r.at[d], to)
        x.start()
        y = remote(b_all.at[me_f], b_all.at[me_f], b_s.at[d], b_r.at[d], to)
        y.start()
        weights_flying += [x, y]

    for p in range(parts):
        for s in range(slots):
            stage_block(1, p, s)
    frecv_a[me_n] = fsend[0, me_n]
    frecv_b[me_n] = fsend[1, me_n]
    second = []
    for d in range(1, parts):
        x = exchange(1, d)
        x.start()
        second.append(x)
    fetch.wait()
    for x in first:
        x.wait()

    order = list(range(fsize - 1, -1, -1))

    def aggregate(c):
        def block(b):
            wcat = jnp.concatenate([tl[b, k] * live(b, k).astype(BF16) for k in range(per_block)], axis=1)
            got = jnp.concatenate(
                [frecv[c][src[k, b] // slots, src[k, b] % slots] for k in range(per_block)], axis=0
            )
            total = jnp.dot(wcat, got, preferred_element_type=F32)
            return (total + feats_in[b, :, column(c)].astype(F32)).astype(BF16)

        lanes = pl.ds(pl.multiple_of(me_f * fw + c * half, half), half)
        sent = []
        for j in order:
            group = flip(me_f, j)

            @pl.loop(0, mine // 4)
            def _(r):
                done = [block(group * mine + r * 4 + i) for i in range(4)]
                for i, got in enumerate(done):
                    if j:
                        to = pl.multiple_of((group * mine + r * 4 + i) * blk, blk)
                        abuf[c, pl.ds(to, blk), :] = got
                    else:
                        agg[pl.ds(pl.multiple_of((r * 4 + i) * blk, blk), blk), lanes] = got

            if j:
                at = pl.ds(pl.multiple_of(group * rows, rows), rows)
                x = remote(abuf.at[c, at, :], agg.at[:, lanes], tr_s.at[c, j], tr_r.at[c, j], (me_n, group))
                x.start()
                sent.append(x)
        return sent

    turned_a = aggregate(0)
    for x in far:
        x.wait()
    for j in range(3, fsize):
        low = j & -j
        if j != low:
            x = pass_on(j - low, low, j)
            x.start()
            weights_flying.append(x)
    for x in second:
        x.wait()
    turned_b = aggregate(1)
    for x in weights_flying:
        x.wait()
    for f in range(fsize):
        b1[:, f * fw : (f + 1) * fw] = b_all[f, :1, :]
        w2t[:, f * fw : (f + 1) * fw] = w2_all[f]
    def depth_half(c, at):
        lhs = jnp.concatenate([agg[at, f * fw + c * half : f * fw + (c + 1) * half] for f in range(fsize)], axis=1)
        rhs = jnp.concatenate([w1[f * fw + c * half : f * fw + (c + 1) * half, :] for f in range(fsize)], axis=0)
        return jnp.dot(lhs, rhs, preferred_element_type=F32)

    for x in turned_a:
        x.wait()

    @pl.loop(0, 4)
    def _(r):
        at = pl.ds(pl.multiple_of(r * width, width), width)
        part[at, :] = depth_half(0, at)

    w2[...] = jnp.concatenate([w2t[...], jnp.zeros((blk - grades, hid), BF16)], axis=0).T
    for x in turned_b:
        x.wait()

    copies = []
    per = width // blk
    for r in range(4):
        at = slice(r * width, (r + 1) * width)
        pre = part[at, :] + depth_half(1, at) + b1[...]
        hb16 = jnp.maximum(pre, 0.0).astype(BF16)
        hidden[at, :] = hb16
        mask[at, :] = jnp.where(pre > 0, 1.0, 0.0).astype(BF16)
        pt = lax.dot_general(w2t[...], hb16, (((1,), (1,)), ((), ())), preferred_element_type=F32)
        for i in range(per):
            pall[base + r * per + i] = pt[:, i * blk : (i + 1) * blk]
        for d in range(1, fsize):
            own = pall.at[pl.ds(base + r * per, per)]
            c = remote(own, own, ag_s.at[r, d], ag_r.at[r, d], (me_n, (me_f + d) % fsize))
            c.start()
            copies.append(c)

    @pl.loop(0, 4)
    def _(r):
        at = pl.ds(pl.multiple_of(r * width, width), width)
        mask_t[:, at] = mask[at, :].T

    for c in copies:
        c.wait()
    for p in range(parts):
        for s in range(slots):
            sbuf[p, s] = pall[table[s, p]]
    rbuf[me_n] = sbuf[me_n]
    copies = []
    for d in range(1, parts):
        p = (me_n + d) % parts
        c = remote(sbuf.at[p], rbuf.at[me_n], ex_s.at[d], ex_r.at[d], (p, me_f))
        c.start()
        copies.append(c)
    for c in copies:
        c.wait()
    for p in range(parts):
        for s in range(slots):
            x = rbuf[p, s]
            hi = x.astype(BF16)
            rest = x - hi.astype(F32)
            mid = rest.astype(BF16)
            low = (rest - mid.astype(F32)).astype(BF16)
            r3[p * slots + s] = jnp.concatenate([hi, mid, low], axis=0)

    grade_id = lax.broadcasted_iota(jnp.int32, (grades, blk), 0)

    @pl.loop(0, mine // 4)
    def _(r):
        four = [r * 4 + i for i in range(4)]
        wcats, outs = [], []
        for b in four:
            pieces = [r3[src[k, base + b]] * live(base + b, k).astype(BF16) for k in range(per_block)]
            lhs = jnp.concatenate(pieces, axis=1)
            wcats.append(jnp.concatenate([tl[base + b, k] for k in range(per_block)], axis=1))
            outs.append(
                lax.dot_general(lhs, wcats[-1], (((1,), (1,)), ((), ())), preferred_element_type=F32)
            )
        dlogs = []
        for b, out in zip(four, outs):
            logits = pall[base + b] + (
                out[:grades] + (out[grades : 2 * grades] + out[2 * grades : 3 * grades])
            )
            expo = jnp.exp(logits)
            probs = expo / jnp.sum(expo, axis=0, keepdims=True)
            onehot = jnp.where(labels[pl.ds(base + b, 1), :] == grade_id, 1.0, 0.0)
            dlogs.append((probs - onehot) * scale)
        backs = [
            jnp.dot(dlog.astype(BF16), wcat, preferred_element_type=F32)
            for dlog, wcat in zip(dlogs, wcats)
        ]
        for b, dlog, back in zip(four, dlogs, backs):
            dl[b] = dlog
            for k in range(per_block):
                contrib[b * per_block + k] = back[:, k * blk : (k + 1) * blk] * live(base + b, k)

    @pl.loop(0, parts)
    def _(p):
        for s in range(slots):
            slot = p * slots + s
            total = jnp.zeros((grades, blk), F32)
            for b in range(mine):
                for k in range(per_block):
                    hit = jnp.where(src[k, base + b] == slot, 1.0, 0.0)
                    total = total + contrib[b * per_block + k] * hit
            sback[p, s] = total.astype(BF16)

    rback[me_n] = sback[me_n]
    copies = []
    for d in range(1, parts):
        p = (me_n + d) % parts
        c = remote(sback.at[p], rback.at[me_n], bk_s.at[d], bk_r.at[d], (p, me_f))
        c.start()
        copies.append(c)
    for c in copies:
        c.wait()

    came = [(rback[p, s].astype(F32), p, s) for p in range(parts) for s in range(slots)]

    @pl.loop(0, nblocks)
    def _(b):
        total = jnp.zeros((grades, blk), F32)
        for x, p, s in came:
            total = total + x * jnp.where(table[s, p] == b, 1.0, 0.0)
        spread[b] = total.astype(BF16)

    copies = []
    for d in range(1, fsize):
        to = (me_f + d) % fsize
        c = remote(
            spread.at[pl.ds(to * mine, mine)], rspread.at[d - 1], sp_s.at[d], sp_r.at[d], (me_n, to)
        )
        c.start()
        copies.append(c)
    for c in copies:
        c.wait()
    for b in range(mine):
        total = spread[base + b].astype(F32)
        for d in range(fsize - 1):
            total = total + rspread[d, b].astype(F32)
        dproj_t[:, b * blk : (b + 1) * blk] = (dl[b] + total).astype(BF16)

    for n in range(parts):
        at = pl.ds(pl.multiple_of(flip(me_n, n) * hb, hb), hb)
        d = jnp.dot(w2[at, :grades], dproj_t[...], preferred_element_type=F32)
        dpre_t[n * hb : (n + 1) * hb, :] = jnp.where(mask_t[at, :] > 0, d, 0.0).astype(BF16)

    orders = stage_bits(parts, fsize)
    stages = len(orders[0])
    sizes = [(fsize * parts) >> (t + 1) for t in range(stages)]
    starts = [sum(sizes[:t]) for t in range(stages)]

    def product(f):
        at = pl.ds(pl.multiple_of(flip(me_f, f) * fw, fw), fw)
        return jnp.dot(dpre_t[...], agg[:, at], preferred_element_type=F32)

    def partner(axis, bit):
        return (flip(me_n, bit), me_f) if axis == "n" else (me_n, flip(me_f, bit))

    def launch(c, t):
        at = pl.ds(starts[t], sizes[t])
        r = remote(gout.at[c, at], gin.at[c, at], rs_s.at[c, t], rs_r.at[c, t], partner(*orders[c][t]))
        r.start()
        return r

    def going(c, t):
        axis, bit = orders[c][t]
        return [j for j in kept(orders[c], t, fsize, parts) if (j[0] if axis == "f" else j[1]) & bit]

    flying = [[], []]
    for f in range(fsize - 1, 0, -2):
        g = product(f).astype(BF16)
        for c in range(2):
            first_tile = (f // 2) * parts
            for n in range(parts):
                gout[c, first_tile + n] = g[n * hb : (n + 1) * hb, c * half : (c + 1) * half]
            at = pl.ds(first_tile, parts)
            r = remote(gout.at[c, at], gin.at[c, at], z_s.at[c, f], z_r.at[c, f], partner("f", 1))
            r.start()
            flying[c].append(r)
    for f in range(fsize):
        if not f & 1:
            g = product(f)
            for c in range(2):
                for n in range(parts):
                    acc[c, f, n] = g[n * hb : (n + 1) * hb, c * half : (c + 1) * half]

    both = jnp.dot(dproj_t[...], hidden[...], preferred_element_type=F32)
    bias = jnp.sum(
        w2t[...].astype(F32) * jnp.dot(dproj_t[...], mask[...], preferred_element_type=F32),
        axis=0,
        keepdims=True,
    )
    small_full = jnp.concatenate([both, jnp.broadcast_to(bias, (8, hid))], axis=0)
    rel = [small_full[:, g * fw : (g + 1) * fw] for g in range(fsize)]
    for f in range(fsize):
        pick = flip(me_f, f)
        total = rel[0]
        for g in range(1, fsize):
            total = jnp.where(pick == g, rel[g], total)
        sm[f] = total

    small_bits = orders[0]
    at_small = 0
    for t in range(stages):
        axis, bit = small_bits[t]
        if axis == "f":
            idx = [f for f in range(fsize) if not f & (bit - 1) and f & bit]
        else:
            idx = [0]
        smalls = []
        for f in idx:
            r = remote(sm.at[f], smin.at[at_small], sm_s.at[at_small], sm_r.at[at_small], partner(axis, bit))
            r.start()
            smalls.append((f - bit if axis == "f" else 0, at_small, r))
            at_small += 1
        for c in range(2):
            for r in flying[c]:
                r.wait()
            sent = going(c, t)
            axis_c, bit_c = orders[c][t]
            for i, j in enumerate(sent):
                k = (j[0] - bit_c, j[1]) if axis_c == "f" else (j[0], j[1] - bit_c)
                new = acc[c, k[0], k[1]] + gin[c, starts[t] + i].astype(F32)
                nxt = going(c, t + 1) if t + 1 < stages else []
                if k in nxt:
                    gout[c, starts[t + 1] + nxt.index(k)] = new.astype(BF16)
                elif t + 1 < stages:
                    acc[c, k[0], k[1]] = new
                else:
                    grad_out[c * half : (c + 1) * half, :] = new.T
            if t + 1 < stages:
                flying[c] = [launch(c, t + 1)]
        for _, _, r in smalls:
            r.wait()
        for f, slot, _ in smalls:
            sm[f] = sm[f] + smin[slot]
    bias_out[...] = sm[0, grades : grades + 1, :]
    second_out[...] = sm[0, :grades, :]


def hand_over(a, b, c, a_out, b_out, c_out):
    a_out[...] = a[...]
    b_out[...] = b[...]
    c_out[...] = c[...]


def shards(features, pair_count, send_blocks, tile_src, tiles, labels, w_first, b_first, w_second):
    nodes, fw = features.shape
    nblocks, per_block = tile_src.shape
    blk = tiles.shape[2]
    parts = lax.axis_size("nodes")
    fsize = lax.axis_size("feat")
    slots = send_blocks.shape[2]
    grades = w_second.shape[1]
    mine = nblocks // fsize
    rows, feats, hid = nodes // fsize, fw * fsize, w_first.shape[1]
    hb = hid // parts
    half = fw // 2
    dims = (parts, fsize, slots, nblocks, per_block, blk, grades, 1.0 / math.sqrt(nodes * parts))
    stages = len(stage_bits(parts, fsize)[0])
    tiles_sent = fsize * parts - 1
    n_small = (fsize - 1) + (parts.bit_length() - 1)
    vm = pl.BlockSpec(memory_space=pltpu.VMEM)
    sc = pl.BlockSpec(memory_space=pltpu.SMEM)
    hbm = pl.BlockSpec(memory_space=pl.ANY)
    dma = pltpu.SemaphoreType.DMA
    field = (grades, blk)
    grad_first, grad_bias, grad_second = pl.pallas_call(
        functools.partial(whole_kernel, dims),
        out_shape=(
            jax.ShapeDtypeStruct((fw, hb), F32),
            jax.ShapeDtypeStruct((1, fw), F32),
            jax.ShapeDtypeStruct((grades, fw), F32),
        ),
        in_specs=[hbm, hbm, vm, vm, hbm, sc, sc, sc, vm],
        out_specs=(vm, vm, vm),
        scratch_shapes=[
            pltpu.VMEM((nblocks, blk, fw), BF16),
            pltpu.VMEM((rows, feats), BF16),
            pltpu.VMEM((feats, hid), BF16),
            pltpu.VMEM((hid, blk), BF16),
            pltpu.VMEM((fsize, grades, fw), BF16),
            pltpu.VMEM((fsize, 8, fw), F32),
            pltpu.VMEM((grades, hid), BF16),
            pltpu.VMEM((1, hid), F32),
            pltpu.VMEM((2, parts, slots, blk, half), BF16),
            pltpu.VMEM((parts, slots, blk, half), BF16),
            pltpu.VMEM((parts, slots, blk, half), BF16),
            pltpu.VMEM((2, nodes, half), BF16),
            pltpu.VMEM((rows, hid), F32),
            pltpu.VMEM((rows, hid), BF16),
            pltpu.VMEM((hid, rows), BF16),
            pltpu.VMEM((rows, hid), BF16),
            pltpu.VMEM((nblocks,) + field, F32),
            pltpu.VMEM((parts, slots) + field, F32),
            pltpu.VMEM((parts, slots) + field, F32),
            pltpu.VMEM((parts * slots, 3 * grades, blk), BF16),
            pltpu.VMEM((nblocks, per_block, blk, blk), BF16),
            pltpu.VMEM((mine,) + field, F32),
            pltpu.VMEM((mine * per_block,) + field, F32),
            pltpu.VMEM((parts, slots) + field, BF16),
            pltpu.VMEM((parts, slots) + field, BF16),
            pltpu.VMEM((nblocks,) + field, BF16),
            pltpu.VMEM((fsize - 1, mine) + field, BF16),
            pltpu.VMEM((grades, rows), BF16),
            pltpu.VMEM((hid, rows), BF16),
            pltpu.VMEM((2, fsize, parts, hb, half), F32),
            pltpu.VMEM((2, tiles_sent, hb, half), BF16),
            pltpu.VMEM((2, tiles_sent, hb, half), BF16),
            pltpu.VMEM((fsize, grades + 8, fw), F32),
            pltpu.VMEM((n_small, grades + 8, fw), F32),
            dma,
            dma,
            dma,
            dma((fsize,)), dma((fsize,)),
            dma((fsize,)), dma((fsize,)),
            dma((fsize,)), dma((fsize,)),
            dma((2, parts)), dma((2, parts)),
            dma((2, fsize)), dma((2, fsize)),
            dma((4, fsize)), dma((4, fsize)),
            dma((parts,)), dma((parts,)),
            dma((parts,)), dma((parts,)),
            dma((fsize,)), dma((fsize,)),
            dma((2, fsize)), dma((2, fsize)),
            dma((2, stages)), dma((2, stages)),
            dma((n_small,)), dma((n_small,)),
        ],
        compiler_params=pltpu.CompilerParams(
            collective_id=1, has_side_effects=True, vmem_limit_bytes=60 * 1024 * 1024
        ),
        cost_estimate=pl.CostEstimate(
            flops=4 * rows * hid * feats, bytes_accessed=6 * rows * hid, transcendentals=rows * grades
        ),
    )(
        features.reshape(nblocks, blk, fw), w_first, b_first[None, :], w_second.T, tiles, tile_src.T,
        pair_count, send_blocks[0].T, labels.reshape(nblocks, blk),
    )
    grad_first, grad_bias, grad_second = pl.pallas_call(
        hand_over,
        out_shape=tuple(jax.ShapeDtypeStruct(x.shape, F32) for x in (grad_first, grad_bias, grad_second)),
        in_specs=[vm, vm, vm],
        out_specs=(vm, vm, vm),
    )(grad_first, grad_bias, grad_second)
    return (grad_first, grad_bias[0], grad_second.T)


def solution(mesh):
    placed = (
        P("nodes", "feat"),
        P("nodes", None),
        P("nodes", None, None),
        P("nodes", None),
        P("nodes", None, None, None),
        P("nodes"),
        P("feat", None),
        P("feat"),
        P("feat", None),
    )
    return jax.shard_map(
        shards,
        mesh=mesh,
        in_specs=placed,
        out_specs=(P("feat", "nodes"), P("feat"), P("feat", None)),
        check_vma=False,
    )
```
